256 devices in a mesh: ctx: 32 (over z, x_hi, core), kvh: 8 (over y, x_lo).
Axes of the slice: x: 4 (x_hi: 2, x_lo: 2; x = x_hi * 2 + x_lo), y: 4, z: 8, core: 2. Of those that a mesh axis runs over, the one named last changes fastest.
Arguments:
- queries: bfloat16 [512, 128, 128], P('ctx', 'kvh'), may hold values from -60 to 60
- cache_keys: bfloat16 [32768, 8, 128], P('ctx', 'kvh'), may hold values from -30 to 30
- cache_values: bfloat16 [32768, 8, 128], P('ctx', 'kvh'), may hold values from -6 to 6
- new_keys: bfloat16 [512, 8, 128], P('ctx', 'kvh'), may hold values from -8 to 8
- new_values: bfloat16 [512, 8, 128], P('ctx', 'kvh'), may hold values from -6 to 6
- fill_rows: int32 [32], P('ctx'), may hold values from 128 to 1024, as said below
- turn_start: int32 [1], replicated, may hold values from 1024 to 4095
- out_weight: bfloat16 [16384, 16384], P('kvh', 'ctx'), may hold values from -0.046875 to 0.046875
Outputs:
- mixed: bfloat16 [512, 16384], P('kvh', 'ctx')
The draws below stay inside these ranges and needn't reach their ends.
Inputs may be any that keep to these rules, and one draw needn't show every extreme that they name: `fill_rows`: each is a multiple of 128; some shard is full.
All inputs are finite; a program needn't handle non-finite values.
Results may differ from the reference program's by a relative error of at most 0.02.
Values may be sent and summed in bfloat16 or wider, within the bound.
No kernel may reach another device: no remote copies, remote signals or barrier semaphores. Data moves between devices by JAX's collectives and lax.ppermute only.
A program may use at most 64 MiB of HBM per device.

```python
import math
import jax
import jax.numpy as jnp
from jax import lax

D = 16384
HD = 128
GROUP = 16
CACHE_DEV = 1024
BLOCK = 128
KV_HEADS = 8
HEADS = 128
TURN = 512
CACHE_ROWS = 32768


def draw_queries(key, part):
    key = jax.random.fold_in(key, 11)
    first_key = jax.random.fold_in(key, 0)
    values = 3.0 * jax.random.truncated_normal(first_key, -6.0, 6.0, (TURN, HEADS, HD), jnp.float32)
    return values.astype(jnp.bfloat16)


def draw_cache_keys(key, part):
    key = jax.random.fold_in(key, 23)
    values = jax.random.truncated_normal(key, -6.0, 6.0, (CACHE_ROWS, KV_HEADS, HD), jnp.float32)
    return values.astype(jnp.bfloat16)


def draw_fill_rows(key, part):
    key = jax.random.fold_in(key, 5)
    first_key, second_key = jax.random.split(key)
    shard_count = CACHE_ROWS // CACHE_DEV
    page_count = CACHE_DEV // BLOCK
    pages = jax.random.randint(first_key, (shard_count,), 1, page_count + 1, dtype=jnp.int32)
    full_shard = jax.random.randint(second_key, (), 0, shard_count, dtype=jnp.int32)
    pages = jnp.where(jnp.arange(shard_count, dtype=jnp.int32) == full_shard, page_count, pages)
    return (pages * BLOCK).astype(jnp.int32)


def block_levels(rng, shape, cuts, low, largest):
    factor_of, own = 1.0, jax.random.fold_in(rng, 6)
    for axis_at, shards_of in cuts:
        heights = jnp.exp(jax.random.uniform(jax.random.fold_in(own, axis_at), (shards_of,), jnp.float32, low / len(cuts), largest / len(cuts)))
        factor_of = factor_of * jnp.repeat(heights, shape[axis_at] // shards_of).reshape([-1 if axis == axis_at else 1 for axis in range(len(shape))])
    return factor_of


def noise(own_key, shape, spread, most, cuts=(), held_as=jnp.bfloat16):
    result = jax.random.normal(own_key, shape, jnp.float32) * spread
    if len(cuts) > 0:
        result = block_levels(own_key, shape, cuts, -0.22, 0.18) * result
    return jnp.clip(result, min=-most, max=most).astype(held_as)


def setup_inputs(seed: int = 0) -> dict:
    key_of = jax.random.split(jax.random.key(seed), 9)
    return {
        "queries": draw_queries(jax.random.fold_in(key_of[8], 71), 0),
        "cache_keys": draw_cache_keys(jax.random.fold_in(key_of[8], 71), 0),
        "cache_values": noise(key_of[2], (CACHE_ROWS, KV_HEADS, HD), 1.0, 6.0, ((0, 32), (1, 8))),
        "new_keys": noise(key_of[3], (TURN, KV_HEADS, HD), 1.4, 8.0, ((0, 32), (1, 8))),
        "new_values": noise(key_of[4], (TURN, KV_HEADS, HD), 1.0, 6.0, ((0, 32), (1, 8))),
        "fill_rows": draw_fill_rows(jax.random.fold_in(key_of[8], 71), 0),
        "turn_start": jax.random.randint(key_of[6], (1,), CACHE_DEV, 4 * CACHE_DEV).astype(jnp.int32),
        "out_weight": noise(key_of[7], (HEADS * HD, D), (HEADS * HD) ** -0.5, 0.046875, ((0, 8), (1, 32))),
    }


NEG = -1e30
ROPE_BASE = 500000.0


def rotate(values, positions):
    half_width = values.shape[-1] // 2
    steps_index = jnp.arange(half_width, dtype=jnp.float32)
    inverse = jnp.exp(steps_index * (-2.0 * math.log(ROPE_BASE) / values.shape[-1]))
    angles = positions[:, None] * inverse[None, :]
    cosine = jnp.cos(angles)[:, None, :]
    sine = jnp.sin(angles)[:, None, :]
    first_half = values[..., :half_width].astype(jnp.float32)
    second_half = values[..., half_width:].astype(jnp.float32)
    return jnp.concatenate([first_half * cosine - second_half * sine, second_half * cosine + first_half * sine], axis=-1).astype(jnp.bfloat16)


def reference(queries, cache_keys, cache_values, new_keys, new_values, fill_rows, turn_start, out_weight):
    token_index = jnp.arange(TURN, dtype=jnp.int32)
    positions = (turn_start[0] + token_index).astype(jnp.float32)
    turned_queries = rotate(queries, positions)
    turned_keys = rotate(new_keys, positions)
    cache_index = jnp.arange(CACHE_ROWS, dtype=jnp.int32)
    live_rows = (cache_index % CACHE_DEV) < fill_rows[cache_index // CACHE_DEV]
    score_scale = HD ** -0.5
    tile_tokens = math.gcd(TURN, 64)
    head_queries = turned_queries.reshape(TURN, KV_HEADS, GROUP, HD).transpose(1, 0, 2, 3)

    def one_head(operands):
        grouped, keys_all, values_all, fresh_keys, fresh_values = operands
        tiles = grouped.reshape(TURN // tile_tokens, tile_tokens * GROUP, HD)
        firsts = jnp.arange(TURN // tile_tokens, dtype=jnp.int32) * tile_tokens

        def one_tile(operand_pair):
            flat_queries, first_row = operand_pair
            cache_scores = jnp.dot(flat_queries, keys_all.T, preferred_element_type=jnp.float32) * score_scale
            cache_scores = jnp.where(live_rows[None, :], cache_scores, NEG)
            query_tokens = first_row + jnp.arange(tile_tokens * GROUP, dtype=jnp.int32) // GROUP
            fresh_scores = jnp.dot(flat_queries, fresh_keys.T, preferred_element_type=jnp.float32) * score_scale
            fresh_scores = jnp.where(token_index[None, :] <= query_tokens[:, None], fresh_scores, NEG)
            row_top = jnp.maximum(cache_scores.max(axis=-1), fresh_scores.max(axis=-1))
            cache_weights = jnp.exp(cache_scores - row_top[:, None]).astype(jnp.bfloat16)
            fresh_weights = jnp.exp(fresh_scores - row_top[:, None]).astype(jnp.bfloat16)
            weight_total = cache_weights.astype(jnp.float32).sum(axis=-1) + fresh_weights.astype(jnp.float32).sum(axis=-1)
            output = jnp.dot(cache_weights, values_all, preferred_element_type=jnp.float32)
            output = output + jnp.dot(fresh_weights, fresh_values, preferred_element_type=jnp.float32)
            return (output / weight_total[:, None]).astype(jnp.bfloat16)

        return lax.map(one_tile, (tiles, firsts)).reshape(TURN, GROUP, HD)

    heads_out = lax.map(one_head, (head_queries, cache_keys.transpose(1, 0, 2), cache_values.transpose(1, 0, 2), turned_keys.transpose(1, 0, 2), new_values.transpose(1, 0, 2)))
    attention = heads_out.transpose(1, 0, 2, 3).reshape(TURN, HEADS * HD)
    return jnp.dot(attention, out_weight, preferred_element_type=jnp.float32).astype(jnp.bfloat16)
```

```python
import functools
import math

import jax
import jax.numpy as jnp
from jax import lax
from jax.experimental import pallas as pl
from jax.experimental.pallas import tpu as pltpu
from jax.sharding import PartitionSpec as P

NEG = -1e30
ROPE_BASE = 500000.0
LOG2E = 1.4426950408889634
HD = 128
STAT = 16
VMEM = pl.BlockSpec(memory_space=pltpu.VMEM)
SMEM = pl.BlockSpec(memory_space=pltpu.SMEM)


def rotate(values, positions):
    half_width = values.shape[-1] // 2
    steps_index = jnp.arange(half_width, dtype=jnp.float32)
    inverse = jnp.exp(steps_index * (-2.0 * math.log(ROPE_BASE) / values.shape[-1]))
    angles = positions[:, None] * inverse[None, :]
    cosine = jnp.cos(angles)[:, None, :]
    sine = jnp.sin(angles)[:, None, :]
    first_half = values[..., :half_width].astype(jnp.float32)
    second_half = values[..., half_width:].astype(jnp.float32)
    return jnp.concatenate(
        [first_half * cosine - second_half * sine, second_half * cosine + first_half * sine],
        axis=-1,
    ).astype(jnp.bfloat16)


def dot_nt(a, b):
    return lax.dot_general(a, b, (((1,), (1,)), ((), ())), preferred_element_type=jnp.float32)


def augment(v_scratch, slot, values):
    v_scratch[slot, :, :HD] = values
    v_scratch[slot, :, HD:] = jnp.ones_like(values)


def fill_bias(pack, cache_rows):
    fill = pack[2 * cache_rows + 32 : 2 * cache_rows + 48, :].astype(jnp.float32)[0:1, :]
    fill = jnp.concatenate([fill] * (cache_rows // HD), axis=1)
    row = lax.broadcasted_iota(jnp.int32, (1, cache_rows), 1).astype(jnp.float32)
    return jnp.where(row < fill, 0.0, NEG)


def first_kernel(chunks, cache_rows, *refs):
    q_refs, (pack_a, pack_b, acc_ref, top_ref, q_all, v_aug) = refs[:chunks], refs[chunks:]
    n = cache_rows
    packs = (pack_a, pack_b)
    for i in range(chunks):
        q_all[i] = q_refs[i][...]
    for s, pack in enumerate(packs):
        augment(v_aug, s, pack[n : 2 * n, :])
    scale = LOG2E / math.sqrt(HD)

    def one_chunk(i, carry):
        q = q_all[i]
        scores = [dot_nt(q, p[0:n, :]) * scale + fill_bias(p, n) for p in packs]
        top = functools.reduce(jnp.maximum, [s.max(axis=1, keepdims=True) for s in scores])
        acc = None
        for s in range(2):
            weights = jnp.exp2(scores[s] - top).astype(jnp.bfloat16)
            part = jnp.dot(weights, v_aug[s], preferred_element_type=jnp.float32)
            acc = part if acc is None else acc + part
        acc_ref[i] = acc
        top_ref[i] = jnp.broadcast_to(top, top_ref.shape[1:])
        return carry

    lax.fori_loop(0, chunks, one_chunk, 0)


def flash_first(q_list, packs, cache_rows):
    chunks = len(q_list)
    rows = q_list[0].shape[0]
    keys = 2 * cache_rows
    return pl.pallas_call(
        functools.partial(first_kernel, chunks, cache_rows),
        out_shape=(
            jax.ShapeDtypeStruct((chunks, rows, 2 * HD), jnp.float32),
            jax.ShapeDtypeStruct((chunks, rows, HD), jnp.float32),
        ),
        in_specs=[VMEM] * (chunks + 2),
        out_specs=(VMEM, VMEM),
        scratch_shapes=[
            pltpu.VMEM((chunks, rows, HD), jnp.bfloat16),
            pltpu.VMEM((2, cache_rows, 2 * HD), jnp.bfloat16),
        ],
        compiler_params=pltpu.CompilerParams(vmem_limit_bytes=36 << 20),
        cost_estimate=pl.CostEstimate(
            flops=chunks * rows * keys * HD * 8,
            bytes_accessed=4 << 20,
            transcendentals=chunks * rows * keys,
        ),
        name="flash_first",
    )(*q_list, *packs)


def second_kernel(half, cache_rows, where_ref, *refs):
    q_refs, refs = refs[: 2 * half], refs[2 * half :]
    acc_a, top_a, acc_b, top_b, pack_o, pack_c, pack_x, pack_xc, out_ref, q_all, v_aug, new_k, new_v = refs
    n = cache_rows
    for i in range(2 * half):
        q_all[i] = q_refs[i][...]
    packs = (pack_x, pack_xc)
    for s, pack in enumerate(packs):
        augment(v_aug, s, pack[n : 2 * n, :])
    new_k[...] = jnp.zeros_like(new_k)
    new_v[...] = jnp.zeros_like(new_v)
    for s, pack in enumerate((pack_o, pack_c, pack_x, pack_xc)):
        new_k[16 * s : 16 * s + 16, :] = pack[2 * n : 2 * n + 16, :]
        new_v[16 * s : 16 * s + 16, :HD] = pack[2 * n + 16 : 2 * n + 32, :]
    new_v[:, HD:] = jnp.ones((HD, HD), jnp.bfloat16)
    scale = LOG2E / math.sqrt(HD)
    rows = q_all.shape[1]
    my_z, my_x, my_c = where_ref[0], where_ref[1], where_ref[2]
    column = lax.broadcasted_iota(jnp.int32, (rows, HD), 1)
    row_token = lax.rem(lax.broadcasted_iota(jnp.int32, (rows, HD), 0), 16)
    key_token = (
        64 * my_z
        + 32 * (my_x ^ (column >> 5))
        + 16 * (my_c ^ ((column >> 4) & 1))
        + (column & 15)
    )
    key_token = jnp.where(column < 64, key_token, 1 << 20)

    def one_chunk(i, acc0, top0):
        q = q_all[i]
        dest = where_ref[3 + i]
        first_token = 64 * dest + 32 * my_x + 16 * my_c
        fresh = dot_nt(q, new_k[...]) * scale
        fresh = jnp.where(key_token <= row_token + first_token, fresh, NEG)
        scores = [dot_nt(q, p[0:n, :]) * scale + fill_bias(p, n) for p in packs]
        top = functools.reduce(
            jnp.maximum, [s.max(axis=1, keepdims=True) for s in scores + [fresh]]
        )
        top = jnp.maximum(top0, jnp.broadcast_to(top, top0.shape))
        one_top = top[:, 0:1]
        keep = jnp.exp2(top0 - top)
        acc = jnp.concatenate([keep, keep], axis=1) * acc0
        for s in range(2):
            weights = jnp.exp2(scores[s] - one_top).astype(jnp.bfloat16)
            acc = acc + jnp.dot(weights, v_aug[s], preferred_element_type=jnp.float32)
        weights = jnp.exp2(fresh - one_top).astype(jnp.bfloat16)
        acc = acc + jnp.dot(weights, new_v[...], preferred_element_type=jnp.float32)
        total = acc[:, HD:]
        out_ref[dest, 0:rows, :] = (acc[:, :HD] / total).astype(jnp.bfloat16)
        level = top + jnp.log2(total)
        stat = jnp.zeros((STAT, HD), jnp.float32)
        line = lax.broadcasted_iota(jnp.int32, (STAT, HD), 0)
        for b in range(rows // HD):
            flat = jnp.transpose(level[b * HD : (b + 1) * HD, :])[0:STAT, :]
            for t in range(3):
                piece = flat.astype(jnp.bfloat16).astype(jnp.float32)
                stat = jnp.where(line == 3 * b + t, piece, stat)
                flat = flat - piece
        out_ref[dest, rows : rows + STAT, :] = stat.astype(jnp.bfloat16)

    def loop_a(i, carry):
        one_chunk(i, acc_a[i], top_a[i])
        return carry

    def loop_b(i, carry):
        one_chunk(i + half, acc_b[i], top_b[i])
        return carry

    lax.fori_loop(0, half, loop_a, 0)
    lax.fori_loop(0, half, loop_b, 0)


def flash_second(where, q_list, state_a, state_b, packs, cache_rows):
    chunks = len(q_list)
    rows = q_list[0].shape[0]
    keys = 2 * cache_rows + HD
    return pl.pallas_call(
        functools.partial(second_kernel, chunks // 2, cache_rows),
        out_shape=jax.ShapeDtypeStruct((chunks, rows + STAT, HD), jnp.bfloat16),
        in_specs=[SMEM] + [VMEM] * (chunks + 8),
        out_specs=VMEM,
        scratch_shapes=[
            pltpu.VMEM((chunks, rows, HD), jnp.bfloat16),
            pltpu.VMEM((2, cache_rows, 2 * HD), jnp.bfloat16),
            pltpu.VMEM((HD, HD), jnp.bfloat16),
            pltpu.VMEM((HD, 2 * HD), jnp.bfloat16),
        ],
        compiler_params=pltpu.CompilerParams(vmem_limit_bytes=36 << 20),
        cost_estimate=pl.CostEstimate(
            flops=chunks * rows * keys * HD * 8,
            bytes_accessed=8 << 20,
            transcendentals=chunks * rows * keys,
        ),
        name="flash_second",
    )(where, *q_list, *state_a, *state_b, *packs)


def merge_kernel(in_ref, out_ref):
    shards = in_ref.shape[0]
    rows = out_ref.shape[0]
    for b in range(rows // HD):
        levels = []
        for s in range(shards):
            stat = in_ref[s, rows : rows + STAT, :].astype(jnp.float32)
            flat = stat[3 * b : 3 * b + 1] + stat[3 * b + 1 : 3 * b + 2] + stat[3 * b + 2 : 3 * b + 3]
            levels.append(jnp.transpose(jnp.broadcast_to(flat, (HD, HD))))
        top = functools.reduce(jnp.maximum, levels)
        total = jnp.zeros((HD, HD), jnp.float32)
        acc = jnp.zeros((HD, HD), jnp.float32)
        for s in range(shards):
            share = jnp.exp2(levels[s] - top)
            total = total + share
            acc = acc + share * in_ref[s, b * HD : (b + 1) * HD, :].astype(jnp.float32)
        out_ref[b * HD : (b + 1) * HD, :] = (acc / total).astype(jnp.bfloat16)


def merge(got):
    rows = got.shape[1] - STAT
    return pl.pallas_call(
        merge_kernel,
        out_shape=jax.ShapeDtypeStruct((rows, HD), jnp.bfloat16),
        in_specs=[VMEM],
        out_specs=VMEM,
        compiler_params=pltpu.CompilerParams(vmem_limit_bytes=16 << 20),
        cost_estimate=pl.CostEstimate(
            flops=4 << 20, bytes_accessed=1 << 20, transcendentals=1 << 18
        ),
        name="merge",
    )(got)


def project_kernel(chunks, where_ref, *refs):
    pair_refs, (w_own, w_core, out_ref, rows_scratch) = refs[:chunks], refs[chunks:]
    my_x = where_ref[1]
    heads = rows_scratch.shape[3] // HD
    for i in range(chunks):
        dest = where_ref[3 + i]
        for k in range(2):
            side = my_x ^ k
            for h in range(heads):
                rows_scratch[dest, side, :, h * HD : (h + 1) * HD] = pair_refs[i][
                    (k * heads + h) * 16 : (k * heads + h) * 16 + 16, :
                ]
    left = rows_scratch[...].reshape(chunks * 32, heads * HD)
    width = w_own.shape[1]
    for k, w in enumerate((w_own, w_core)):
        terms = jnp.dot(left, w[...], preferred_element_type=jnp.float32)
        out_ref[:, :, k * width : (k + 1) * width] = terms.astype(jnp.bfloat16).reshape(
            chunks, 32, width
        )


def project(where, pairs, w_own, w_core):
    chunks = len(pairs)
    depth, width = w_own.shape
    return pl.pallas_call(
        functools.partial(project_kernel, chunks),
        out_shape=jax.ShapeDtypeStruct((chunks, 32, 2 * width), jnp.bfloat16),
        in_specs=[SMEM] + [VMEM] * (chunks + 2),
        out_specs=VMEM,
        scratch_shapes=[pltpu.VMEM((chunks, 2, 16, depth), jnp.bfloat16)],
        compiler_params=pltpu.CompilerParams(vmem_limit_bytes=24 << 20),
        cost_estimate=pl.CostEstimate(
            flops=2 * chunks * 32 * depth * 2 * width, bytes_accessed=6 << 20, transcendentals=0
        ),
        name="project",
    )(where, *pairs, w_own, w_core)


ORDER = (0, 1, 7, 2, 6, 3, 5, 4)


def on_device(
    queries, cache_keys, cache_values, new_keys, new_values, fill_rows, turn_start, out_weight
):
    tok_dev, group_size, head_width = queries.shape
    ctx_count = lax.axis_size("ctx")
    z_count = ctx_count // 4
    kvh_count = lax.axis_size("kvh")
    me = lax.axis_index("ctx")
    my_z, my_x, my_c = me // 4, (me // 2) % 2, me % 2
    cache_rows = cache_keys.shape[0]

    def permutation(target):
        return [
            ((z * 2 + x) * 2 + c, (target(z, x, c)[0] * 2 + target(z, x, c)[1]) * 2 + target(z, x, c)[2])
            for z in range(z_count)
            for x in range(2)
            for c in range(2)
        ]

    to_core = permutation(lambda z, x, c: (z, x, 1 - c))
    to_x = permutation(lambda z, x, c: (z, 1 - x, c))
    to_up = permutation(lambda z, x, c: ((z + 1) % z_count, x, c))
    to_down = permutation(lambda z, x, c: ((z - 1) % z_count, x, c))

    def send(value, where_to):
        return lax.ppermute(value, "ctx", where_to)

    def ring(own):
        by_offset = {0: own}
        from_below, from_above = own, own
        for step in range(1, z_count // 2 + 1):
            from_below = send(from_below, to_up)
            by_offset[z_count - step] = from_below
            if step < z_count // 2:
                from_above = send(from_above, to_down)
                by_offset[step] = from_above
        return [by_offset[d] for d in ORDER]

    positions = (turn_start[0] + me * tok_dev + jnp.arange(tok_dev, dtype=jnp.int32)).astype(
        jnp.float32
    )
    own_queries = (
        rotate(queries, positions).transpose(1, 0, 2).reshape(group_size * tok_dev, head_width)
    )
    turned_keys = rotate(new_keys, positions).reshape(tok_dev, head_width)
    fill_block = jnp.full((16, head_width), fill_rows[0].astype(jnp.bfloat16))
    pack = jnp.concatenate(
        [
            cache_keys.reshape(cache_rows, head_width),
            cache_values.reshape(cache_rows, head_width),
            turned_keys,
            new_values.reshape(tok_dev, head_width),
            fill_block,
        ],
        axis=0,
    )
    pack_x = send(pack, to_x)
    pack_c = send(pack, to_core)
    pack_xc = send(pack_x, to_core)
    w_core = send(out_weight, to_core)
    where = jnp.concatenate(
        [
            jnp.stack([my_z, my_x, my_c]),
            (my_z + jnp.asarray(ORDER, jnp.int32)) % z_count,
        ]
    ).astype(jnp.int32)

    gathered = ring(own_queries)
    half = z_count // 2
    state_a = flash_first(gathered[:half], (pack, pack_c), cache_rows)
    state_b = flash_first(gathered[half:], (pack, pack_c), cache_rows)
    partial = flash_second(
        where, gathered, state_a, state_b, (pack, pack_c, pack_x, pack_xc), cache_rows
    )
    z_groups = [
        [(z * 2 + x) * 2 + c for z in range(z_count)] for x in range(2) for c in range(2)
    ]
    got = lax.all_to_all(partial, "ctx", 0, 0, axis_index_groups=z_groups, tiled=True)
    attention = merge(got)
    pair = jnp.concatenate([attention, send(attention, to_x)], axis=0)
    pairs = ring(pair)
    terms = project(where, pairs, out_weight, w_core)
    summed = (
        lax.all_to_all(terms, "kvh", 0, 0, tiled=True)
        .astype(jnp.float32)
        .sum(axis=0)
        .astype(jnp.bfloat16)
    )
    width = out_weight.shape[1]
    mine = summed[:, :width].reshape(2, 1, tok_dev, width)
    other = send(summed[:, width:], to_core).reshape(2, 1, tok_dev, width)
    ordered = jnp.where(
        my_c == 0,
        jnp.concatenate([mine, other], axis=1),
        jnp.concatenate([other, mine], axis=1),
    )
    return ordered.reshape(4 * tok_dev, width)


def solution(mesh):
    in_specs = (
        P("ctx", "kvh", None),
        P("ctx", "kvh", None),
        P("ctx", "kvh", None),
        P("ctx", "kvh", None),
        P("ctx", "kvh", None),
        P("ctx"),
        P(),
        P("kvh", "ctx"),
    )
    out_specs = P("kvh", "ctx")
    return jax.shard_map(
        on_device, mesh=mesh, in_specs=in_specs, out_specs=out_specs, check_vma=False
    )
```

```python
import functools
import math

import jax
import jax.numpy as jnp
from jax import lax
from jax.experimental import pallas as pl
from jax.experimental.pallas import tpu as pltpu
from jax.sharding import PartitionSpec as P

NEG = -1e30
ROPE_BASE = 500000.0
LOG2E = 1.4426950408889634
HD = 128
STAT = 16
VMEM = pl.BlockSpec(memory_space=pltpu.VMEM)
SMEM = pl.BlockSpec(memory_space=pltpu.SMEM)


def rotate(values, positions):
    half_width = values.shape[-1] // 2
    steps_index = jnp.arange(half_width, dtype=jnp.float32)
    inverse = jnp.exp(steps_index * (-2.0 * math.log(ROPE_BASE) / values.shape[-1]))
    angles = positions[:, None] * inverse[None, :]
    cosine = jnp.cos(angles)[:, None, :]
    sine = jnp.sin(angles)[:, None, :]
    first_half = values[..., :half_width].astype(jnp.float32)
    second_half = values[..., half_width:].astype(jnp.float32)
    return jnp.concatenate(
        [first_half * cosine - second_half * sine, second_half * cosine + first_half * sine],
        axis=-1,
    ).astype(jnp.bfloat16)


def dot_nt(a, b):
    return lax.dot_general(a, b, (((1,), (1,)), ((), ())), preferred_element_type=jnp.float32)


def fill_bias(note, cache_rows):
    fill = note[32:48, :].astype(jnp.float32)[0:1, :]
    fill = jnp.concatenate([fill] * (cache_rows // HD), axis=1)
    row = lax.broadcasted_iota(jnp.int32, (1, cache_rows), 1).astype(jnp.float32)
    return jnp.where(row < fill, 0.0, NEG)


def absorb(state, scores, values):
    weigh = jnp.concatenate([values, jnp.ones_like(values)], axis=1)
    high = scores.max(axis=1, keepdims=True)
    if state is None:
        weights = jnp.exp2(scores - high).astype(jnp.bfloat16)
        return high, jnp.dot(weights, weigh, preferred_element_type=jnp.float32)
    top, acc = state
    high = jnp.maximum(top, high)
    weights = jnp.exp2(scores - high).astype(jnp.bfloat16)
    term = jnp.dot(weights, weigh, preferred_element_type=jnp.float32)
    return high, acc * jnp.exp2(top - high) + term


def sweep(states, tiles, sources):
    scale = LOG2E / math.sqrt(HD)
    for keys, values, note in sources:
        n = keys.shape[0]
        block = min(512, n)
        bias = fill_bias(note, n)
        for b in range(0, n, block):
            for t, q in enumerate(tiles):
                scores = dot_nt(q, keys[b : b + block, :]) * scale + bias[:, b : b + block]
                states[t] = absorb(states[t], scores, values[b : b + block, :])
    return states


def tile_groups(q_refs):
    whole = q_refs[0].shape[0]
    even = len(q_refs) // 2 * 2
    groups = [((i, 0, whole), (i + 1, 0, whole)) for i in range(0, even, 2)]
    if even < len(q_refs):
        groups.append(((even, 0, whole // 2), (even, whole // 2, whole // 2)))
    return groups


def first_kernel(chunks, *refs):
    q_refs, refs = refs[:chunks], refs[chunks:]
    sources, (acc_ref, top_ref) = (refs[0:3], refs[3:6]), refs[6:]
    for group in tile_groups(q_refs):
        tiles = [q_refs[i][p : p + rows, :] for i, p, rows in group]
        states = sweep([None] * len(tiles), tiles, sources)
        for (i, p, rows), (top, acc) in zip(group, states):
            acc_ref[i, p : p + rows, :] = acc
            top_ref[i, p : p + rows, :] = jnp.broadcast_to(top, (rows, HD))


def flash_first(q_list, sources):
    chunks, rows = len(q_list), q_list[0].shape[0]
    keys = sum(source[0].shape[0] for source in sources)
    return pl.pallas_call(
        functools.partial(first_kernel, chunks),
        out_shape=(
            jax.ShapeDtypeStruct((chunks, rows, 2 * HD), jnp.float32),
            jax.ShapeDtypeStruct((chunks, rows, HD), jnp.float32),
        ),
        in_specs=[VMEM] * (chunks + 6),
        out_specs=(VMEM, VMEM),
        compiler_params=pltpu.CompilerParams(vmem_limit_bytes=14 << 20),
        cost_estimate=pl.CostEstimate(
            flops=chunks * rows * keys * HD * 8,
            bytes_accessed=2 << 20,
            transcendentals=chunks * rows * keys,
        ),
        name="flash_first",
    )(*q_list, *sources[0], *sources[1])


def pack_level(level, stat, first_row):
    line = lax.broadcasted_iota(jnp.int32, stat.shape, 0)
    for b in range(level.shape[0] // HD):
        flat = jnp.transpose(level[b * HD : (b + 1) * HD, :])[0:STAT, :]
        for t in range(3):
            piece = flat.astype(jnp.bfloat16).astype(jnp.float32)
            stat = jnp.where(line == 3 * (first_row // HD + b) + t, piece, stat)
            flat = flat - piece
    return stat


def second_kernel(offsets, shards, where_ref, *refs):
    chunks = len(offsets)
    q_refs, refs = refs[:chunks], refs[chunks:]
    acc_ref, top_ref, sources, notes = refs[0], refs[1], (refs[2:5], refs[5:8]), refs[8:10]
    out_refs, (new_k, new_v) = refs[10 : 10 + chunks], refs[10 + chunks :]
    notes = notes + (sources[0][2], sources[1][2])
    new_k[...] = jnp.zeros_like(new_k)
    new_v[...] = jnp.zeros_like(new_v)
    for s, note in enumerate(notes):
        new_k[16 * s : 16 * s + 16, :] = note[0:16, :]
        new_v[16 * s : 16 * s + 16, :] = note[16:32, :]
    scale = LOG2E / math.sqrt(HD)
    my_z, my_x, my_c = where_ref[0], where_ref[1], where_ref[2]
    column = lax.broadcasted_iota(jnp.int32, (1, HD), 1)
    key_token = (
        64 * my_z
        + 32 * (my_x ^ (column >> 5))
        + 16 * (my_c ^ ((column >> 4) & 1))
        + (column & 15)
    )
    key_token = jnp.where(column < 64, key_token, 1 << 20)
    stats = [jnp.zeros((STAT, HD), jnp.float32) for _ in q_refs]
    for group in tile_groups(q_refs):
        tiles = [q_refs[i][p : p + rows, :] for i, p, rows in group]
        states = []
        for tile, (i, p, rows) in zip(tiles, group):
            home = lax.rem(my_z + offsets[i] + shards, shards)
            row_token = lax.broadcasted_iota(jnp.int32, (rows, HD), 0) & 15
            row_token = row_token + (64 * home + 32 * my_x + 16 * my_c)
            scores = dot_nt(tile, new_k[...]) * scale
            scores = jnp.where(key_token <= row_token, scores, NEG)
            state = (top_ref[i, p : p + rows, :][:, 0:1], acc_ref[i, p : p + rows, :])
            states.append(absorb(state, scores, new_v[...]))
        states = sweep(states, tiles, sources)
        for (i, p, rows), (top, acc) in zip(group, states):
            total = acc[:, HD:]
            out_refs[i][p : p + rows, :] = (acc[:, :HD] / total).astype(jnp.bfloat16)
            stats[i] = pack_level(top + jnp.log2(total), stats[i], p)
    for i, out in enumerate(out_refs):
        whole = q_refs[i].shape[0]
        out[whole : whole + STAT, :] = stats[i].astype(jnp.bfloat16)


def flash_second(where, offsets, shards, q_list, state, sources, notes):
    chunks, rows = len(q_list), q_list[0].shape[0]
    keys = sum(source[0].shape[0] for source in sources) + HD
    return pl.pallas_call(
        functools.partial(second_kernel, offsets, shards),
        out_shape=[jax.ShapeDtypeStruct((rows + STAT, HD), jnp.bfloat16)] * chunks,
        in_specs=[SMEM] + [VMEM] * (chunks + 10),
        out_specs=[VMEM] * chunks,
        scratch_shapes=[pltpu.VMEM((HD, HD), jnp.bfloat16), pltpu.VMEM((HD, HD), jnp.bfloat16)],
        compiler_params=pltpu.CompilerParams(vmem_limit_bytes=14 << 20),
        cost_estimate=pl.CostEstimate(
            flops=chunks * rows * keys * HD * 8,
            bytes_accessed=2 << 20,
            transcendentals=chunks * rows * keys,
        ),
        name="flash_second",
    )(where, *q_list, *state, *sources[0], *sources[1], *notes)


def merge_kernel(final, *refs):
    in_refs, out_ref = refs[:-1], refs[-1]
    rows = in_refs[0].shape[0] - STAT
    packed = jnp.zeros((STAT, HD), jnp.float32)
    for b in range(rows // HD):
        levels = []
        for part in in_refs:
            stat = part[rows : rows + STAT, :].astype(jnp.float32)
            flat = stat[3 * b : 3 * b + 1] + stat[3 * b + 1 : 3 * b + 2] + stat[3 * b + 2 : 3 * b + 3]
            levels.append(jnp.transpose(jnp.broadcast_to(flat, (HD, HD))))
        top = functools.reduce(jnp.maximum, levels)
        total = jnp.zeros((HD, HD), jnp.float32)
        acc = jnp.zeros((HD, HD), jnp.float32)
        for part, level in zip(in_refs, levels):
            share = jnp.exp2(level - top)
            total = total + share
            acc = acc + share * part[b * HD : (b + 1) * HD, :].astype(jnp.float32)
        out_ref[b * HD : (b + 1) * HD, :] = (acc / total).astype(jnp.bfloat16)
        packed = pack_level(top + jnp.log2(total), packed, b * HD)
    if not final:
        out_ref[rows : rows + STAT, :] = packed.astype(jnp.bfloat16)


def merge(parts, final):
    rows = parts[0].shape[0] - (STAT if final else 0)
    return pl.pallas_call(
        functools.partial(merge_kernel, final),
        out_shape=jax.ShapeDtypeStruct((rows, HD), jnp.bfloat16),
        in_specs=[VMEM] * len(parts),
        out_specs=VMEM,
        compiler_params=pltpu.CompilerParams(vmem_limit_bytes=12 << 20),
        cost_estimate=pl.CostEstimate(
            flops=4 << 20, bytes_accessed=1 << 20, transcendentals=1 << 18
        ),
        name="merge",
    )(*parts)


def project_kernel(chunks, where_ref, *refs):
    pair_refs, (w_own, w_core, out_ref, left_ref) = refs[:chunks], refs[chunks:]
    my_z, my_x = where_ref[0], where_ref[1]
    heads = left_ref.shape[3] // HD
    for i in range(chunks):
        home = lax.rem(my_z + i, chunks)
        for k in range(2):
            for h in range(heads):
                first = (k * heads + h) * 16
                left_ref[home, my_x ^ k, :, h * HD : (h + 1) * HD] = pair_refs[i][
                    first : first + 16, :
                ]
    left = left_ref[...].reshape(chunks * 32, heads * HD)
    width = w_own.shape[1]
    for k, w in enumerate((w_own, w_core)):
        terms = jnp.dot(left, w[...], preferred_element_type=jnp.float32)
        out_ref[:, :, k * width : (k + 1) * width] = terms.astype(jnp.bfloat16).reshape(
            chunks, 32, width
        )


def project(where, pairs, w_own, w_core):
    chunks = len(pairs)
    depth, width = w_own.shape
    return pl.pallas_call(
        functools.partial(project_kernel, chunks),
        out_shape=jax.ShapeDtypeStruct((chunks, 32, 2 * width), jnp.bfloat16),
        in_specs=[SMEM] + [VMEM] * (chunks + 2),
        out_specs=VMEM,
        scratch_shapes=[pltpu.VMEM((chunks, 2, 16, depth), jnp.bfloat16)],
        compiler_params=pltpu.CompilerParams(vmem_limit_bytes=14 << 20),
        cost_estimate=pl.CostEstimate(
            flops=2 * chunks * 32 * depth * 2 * width, bytes_accessed=6 << 20, transcendentals=0
        ),
        name="project",
    )(where, *pairs, w_own, w_core)


def on_device(
    queries, cache_keys, cache_values, new_keys, new_values, fill_rows, turn_start, out_weight
):
    tok_dev, group_size, head_width = queries.shape
    ctx_count = lax.axis_size("ctx")
    shards = ctx_count // 4
    me = lax.axis_index("ctx")
    my_z, my_x, my_c = me // 4, (me // 2) % 2, me % 2
    cache_rows = cache_keys.shape[0]

    def permutation(dz, dx, dc):
        place = lambda z, x, c: ((z % shards) * 2 + x) * 2 + c
        return [
            (place(z, x, c), place(z + dz, x ^ dx, c ^ dc))
            for z in range(shards)
            for x in range(2)
            for c in range(2)
        ]

    def send(value, dz=0, dx=0, dc=0):
        return lax.ppermute(value, "ctx", permutation(dz, dx, dc))

    def after(value, *others):
        return lax.optimization_barrier((value,) + others)[0]

    keys = cache_keys.reshape(cache_rows, head_width)
    values = cache_values.reshape(cache_rows, head_width)
    keys_x, values_x = send(keys, dx=1), send(values, dx=1)
    keys_c, values_c = send(keys, dc=1), send(values, dc=1)
    positions = (turn_start[0] + me * tok_dev + jnp.arange(tok_dev, dtype=jnp.int32)).astype(
        jnp.float32
    )
    where = jnp.stack([my_z, my_x, my_c]).astype(jnp.int32)
    q = {}
    q[0] = rotate(queries, positions).transpose(1, 0, 2).reshape(group_size * tok_dev, head_width)
    for d in (1, -1, 2, -2):
        q[d] = send(q[0], dz=-d)
    note = jnp.concatenate(
        [
            rotate(new_keys, positions).reshape(tok_dev, head_width),
            new_values.reshape(tok_dev, head_width),
            jnp.full((16, head_width), fill_rows[0].astype(jnp.bfloat16)),
        ],
        axis=0,
    )
    note_c, note_x = send(note, dc=1), send(note, dx=1)
    near = ((keys, values, note), (keys_c, values_c, note_c))
    here, wide, outer = (0,), (1, -1, 2, -2), (3, -3, 4)
    state = {here: flash_first([q[0]], near)}
    up, down = after(q[2], state[here][1]), after(q[-2], state[here][1])
    q[3], q[-3], q[4] = send(up, dz=-1), send(down, dz=1), send(up, dz=-2)
    state[wide] = flash_first([q[d] for d in wide], near)
    keys_x, values_x = after(keys_x, state[wide][1]), after(values_x, state[wide][1])
    keys_xc, values_xc, note_xc = send(keys_x, dc=1), send(values_x, dc=1), send(note_x, dc=1)
    state[outer] = flash_first([q[d] for d in outer], near)
    far = ((keys_x, values_x, note_x), (keys_xc, values_xc, note_xc))

    def finish(offsets):
        done = flash_second(
            where, offsets, shards, [q[d] for d in offsets], state[offsets], far, (note, note_c)
        )
        return dict(zip(offsets, done))

    part = finish(outer)
    from_3, from_4, from_m3 = send(part[3], dz=1), send(part[4], dz=2), send(part[-3], dz=-1)
    w_core = send(after(out_weight, part[4]), dc=1)
    part.update(finish(wide))
    got = [send(part[1], dz=1), send(part[-1], dz=-1)]
    up, down = merge([part[2], from_3, from_4], False), merge([part[-2], from_m3], False)
    got += [send(up, dz=2), send(down, dz=-2)]
    q[0] = after(q[0], up, down)
    part.update(finish(here))
    attention = merge([part[0]] + got, True)

    pair = {0: jnp.concatenate([attention, send(attention, dx=1)], axis=0)}
    for d in (1, -1, 2, -2):
        pair[d] = send(pair[0], dz=-d)
    pair[3], pair[-3], pair[4] = send(pair[2], dz=-1), send(pair[-2], dz=1), send(pair[2], dz=-2)
    terms = project(where, [pair[d if d <= 4 else d - 8] for d in range(8)], out_weight, w_core)
    summed = (
        lax.all_to_all(terms, "kvh", 0, 0, tiled=True)
        .astype(jnp.float32)
        .sum(axis=0)
        .astype(jnp.bfloat16)
    )
    width = out_weight.shape[1]
    mine = summed[:, :width].reshape(2, 1, tok_dev, width)
    other = send(summed[:, width:], dc=1).reshape(2, 1, tok_dev, width)
    ordered = jnp.where(
        my_c == 0,
        jnp.concatenate([mine, other], axis=1),
        jnp.concatenate([other, mine], axis=1),
    )
    return ordered.reshape(4 * tok_dev, width)


def solution(mesh):
    in_specs = (
        P("ctx", "kvh", None),
        P("ctx", "kvh", None),
        P("ctx", "kvh", None),
        P("ctx", "kvh", None),
        P("ctx", "kvh", None),
        P("ctx"),
        P(),
        P("kvh", "ctx"),
    )
    out_specs = P("kvh", "ctx")
    return jax.shard_map(
        on_device, mesh=mesh, in_specs=in_specs, out_specs=out_specs, check_vma=False
    )
```

```python
import functools
import math

import jax
import jax.numpy as jnp
from jax import lax
from jax.experimental import pallas as pl
from jax.experimental.pallas import tpu as pltpu
from jax.sharding import PartitionSpec as P

NEG = -1e30
ROPE_BASE = 500000.0
LOG2E = 1.4426950408889634
HD = 128
STAT = 16
VMEM = pl.BlockSpec(memory_space=pltpu.VMEM)
HBM = pl.BlockSpec(memory_space=pltpu.HBM)


def prepare_kernel(q_hbm, k_hbm, v_hbm, fresh, cosine, sine, q_out, pack_out, q_in, turned, sems):
    n = k_hbm.shape[0]
    piece = n // 4
    copies = [pltpu.make_async_copy(q_hbm, q_in, sems.at[0])]
    for i in range(8):
        source = (k_hbm, v_hbm)[i // 4].at[i % 4 * piece : (i % 4 + 1) * piece]
        target = pack_out.at[i * piece : (i + 1) * piece]
        copies.append(pltpu.make_async_copy(source, target, sems.at[1 + i]))
    for copy in copies:
        copy.start()
    cos, sin = cosine[...], sine[...]
    new_k = fresh[0:16, :].astype(jnp.float32)
    new_k = new_k * cos + pltpu.roll(new_k, HD // 2, 1) * sin
    pack_out[2 * n : 2 * n + 16, :] = new_k.astype(jnp.bfloat16)
    pack_out[2 * n + 16 : 2 * n + NOTE, :] = fresh[16:NOTE, :]
    copies[0].wait()
    tokens, heads, width = q_in.shape
    old = q_in[...].astype(jnp.float32)
    swapped = pltpu.roll(old.reshape(tokens * heads, width), HD // 2, 1).reshape(old.shape)
    turned[...] = old * cos[:, None, :] + swapped * sin[:, None, :]
    for h in range(heads):
        q_out[tokens * h : tokens * (h + 1), :] = turned[:, h, :].astype(jnp.bfloat16)
    for copy in copies[1:]:
        copy.wait()


def prepare(queries, keys, values, fresh, positions):
    tokens, heads, width = queries.shape
    steps_index = jnp.arange(width // 2, dtype=jnp.float32)
    inverse = jnp.exp(steps_index * (-2.0 * math.log(ROPE_BASE) / width))
    angles = positions[:, None] * jnp.concatenate([inverse, inverse])[None, :]
    sign = jnp.where(jnp.arange(width) < width // 2, -1.0, 1.0).astype(jnp.float32)
    n = keys.shape[0]
    return pl.pallas_call(
        prepare_kernel,
        out_shape=(
            jax.ShapeDtypeStruct((tokens * heads, width), jnp.bfloat16),
            jax.ShapeDtypeStruct((2 * n + NOTE, width), jnp.bfloat16),
        ),
        in_specs=[HBM] * 3 + [VMEM] * 3,
        out_specs=(VMEM, VMEM),
        scratch_shapes=[
            pltpu.VMEM(queries.shape, jnp.bfloat16),
            pltpu.VMEM(queries.shape, jnp.float32),
            pltpu.SemaphoreType.DMA((9,)),
        ],
        compiler_params=pltpu.CompilerParams(vmem_limit_bytes=12 << 20),
        cost_estimate=pl.CostEstimate(flops=1 << 18, bytes_accessed=1 << 20, transcendentals=0),
        name="prepare",
    )(queries, keys, values, fresh, jnp.cos(angles), jnp.sin(angles) * sign)


def dot_nt(a, b):
    return lax.dot_general(a, b, (((1,), (1,)), ((), ())), preferred_element_type=jnp.float32)


NOTE = 48


def fill_bias(pack, n):
    fill = pack[2 * n + 32 : 2 * n + 48, :].astype(jnp.float32)[0:1, :]
    fill = jnp.concatenate([fill] * (n // HD), axis=1)
    row = lax.broadcasted_iota(jnp.int32, (1, n), 1).astype(jnp.float32)
    return jnp.where(row < fill, 0.0, NEG)


def absorb(state, scores, values):
    weigh = jnp.concatenate([values, jnp.ones_like(values)], axis=1)
    high = scores.max(axis=1, keepdims=True)
    if state is None:
        weights = jnp.exp2(scores - high).astype(jnp.bfloat16)
        return high, jnp.dot(weights, weigh, preferred_element_type=jnp.float32)
    top, acc = state
    high = jnp.maximum(top, high)
    weights = jnp.exp2(scores - high).astype(jnp.bfloat16)
    term = jnp.dot(weights, weigh, preferred_element_type=jnp.float32)
    return high, acc * jnp.exp2(top - high) + term


def sweep(states, tiles, packs):
    scale = LOG2E / math.sqrt(HD)
    for pack in packs:
        n = (pack.shape[0] - NOTE) // 2
        block = min(512, n)
        bias = fill_bias(pack, n)
        for b in range(0, n, block):
            for t, q in enumerate(tiles):
                scores = dot_nt(q, pack[b : b + block, :]) * scale + bias[:, b : b + block]
                states[t] = absorb(states[t], scores, pack[n + b : n + b + block, :])
    return states


def tile_groups(q_refs):
    whole = q_refs[0].shape[0]
    even = len(q_refs) // 2 * 2
    groups = [((i, 0, whole), (i + 1, 0, whole)) for i in range(0, even, 2)]
    if even < len(q_refs):
        groups.append(((even, 0, whole // 2), (even, whole // 2, whole // 2)))
    return groups


def first_kernel(chunks, *refs):
    q_refs, refs = refs[:chunks], refs[chunks:]
    packs, (acc_ref, top_ref) = refs[0:2], refs[2:]
    for group in tile_groups(q_refs):
        tiles = [q_refs[i][p : p + rows, :] for i, p, rows in group]
        states = sweep([None] * len(tiles), tiles, packs)
        for (i, p, rows), (top, acc) in zip(group, states):
            acc_ref[i, p : p + rows, :] = acc
            top_ref[i, p : p + rows, :] = jnp.broadcast_to(top, (rows, HD))


def flash_first(q_list, packs):
    chunks, rows = len(q_list), q_list[0].shape[0]
    keys = sum(pack.shape[0] - NOTE for pack in packs) // 2
    return pl.pallas_call(
        functools.partial(first_kernel, chunks),
        out_shape=(
            jax.ShapeDtypeStruct((chunks, rows, 2 * HD), jnp.float32),
            jax.ShapeDtypeStruct((chunks, rows, HD), jnp.float32),
        ),
        in_specs=[VMEM] * (chunks + 2),
        out_specs=(VMEM, VMEM),
        compiler_params=pltpu.CompilerParams(vmem_limit_bytes=14 << 20),
        cost_estimate=pl.CostEstimate(
            flops=chunks << 29, bytes_accessed=1 << 20, transcendentals=0
        ),
        name="flash_first",
    )(*q_list, *packs)


def pack_level(level, stat, first_row):
    line = lax.broadcasted_iota(jnp.int32, stat.shape, 0)
    for b in range(level.shape[0] // HD):
        flat = jnp.transpose(level[b * HD : (b + 1) * HD, :])[0:STAT, :]
        for t in range(3):
            piece = flat.astype(jnp.bfloat16).astype(jnp.float32)
            stat = jnp.where(line == 3 * (first_row // HD + b) + t, piece, stat)
            flat = flat - piece
    return stat


def place():
    me = lax.axis_index("ctx")
    return me >> 2, (me >> 1) & 1, me & 1


def second_kernel(offsets, shards, first, *refs):
    chunks = len(offsets)
    q_refs, refs = refs[:chunks], refs[chunks:]
    acc_ref, top_ref, packs = refs[0], refs[1], refs[2:6]
    out_refs, (new_k, new_v) = refs[6 : 6 + chunks], refs[6 + chunks :]
    n = (packs[0].shape[0] - NOTE) // 2
    new_k[...] = jnp.zeros_like(new_k)
    new_v[...] = jnp.zeros_like(new_v)
    for s, pack in enumerate(packs):
        new_k[16 * s : 16 * s + 16, :] = pack[2 * n : 2 * n + 16, :]
        new_v[16 * s : 16 * s + 16, :] = pack[2 * n + 16 : 2 * n + 32, :]
    scale = LOG2E / math.sqrt(HD)
    my_z, my_x, my_c = place()
    column = lax.broadcasted_iota(jnp.int32, (1, HD), 1)
    key_token = (
        64 * my_z
        + 32 * (my_x ^ (column >> 5))
        + 16 * (my_c ^ ((column >> 4) & 1))
        + (column & 15)
    )
    key_token = jnp.where(column < 64, key_token, 1 << 20)
    stats = [jnp.zeros((STAT, HD), jnp.float32) for _ in q_refs]
    for group in tile_groups(q_refs):
        tiles = [q_refs[i][p : p + rows, :] for i, p, rows in group]
        states = []
        for tile, (i, p, rows) in zip(tiles, group):
            home = lax.rem(my_z + offsets[i] + shards, shards)
            row_token = lax.broadcasted_iota(jnp.int32, (rows, HD), 0) & 15
            row_token = row_token + (64 * home + 32 * my_x + 16 * my_c)
            scores = dot_nt(tile, new_k[...]) * scale
            scores = jnp.where(key_token <= row_token, scores, NEG)
            states.append(absorb(None, scores, new_v[...]))
        states = sweep(states, tiles, packs[2:])
        for (i, p, rows), (top, acc) in zip(group, states):
            near_top = top_ref[first + i, p : p + rows, :]
            top = jnp.broadcast_to(top, near_top.shape)
            high = jnp.maximum(top, near_top)
            near, far = jnp.exp2(near_top - high), jnp.exp2(top - high)
            near_acc = acc_ref[first + i, p : p + rows, :]
            total = near * near_acc[:, HD:] + far * acc[:, HD:]
            mean = (near * near_acc[:, :HD] + far * acc[:, :HD]) / total
            out_refs[i][p : p + rows, :] = mean.astype(jnp.bfloat16)
            stats[i] = pack_level(high + jnp.log2(total), stats[i], p)
    for i, out in enumerate(out_refs):
        whole = q_refs[i].shape[0]
        out[whole : whole + STAT, :] = stats[i].astype(jnp.bfloat16)


def flash_second(offsets, shards, q_list, state, first, packs):
    chunks, rows = len(q_list), q_list[0].shape[0]
    keys = packs[0].shape[0]
    return pl.pallas_call(
        functools.partial(second_kernel, offsets, shards, first),
        out_shape=[jax.ShapeDtypeStruct((rows + STAT, HD), jnp.bfloat16)] * chunks,
        in_specs=[VMEM] * (chunks + 6),
        out_specs=[VMEM] * chunks,
        scratch_shapes=[pltpu.VMEM((HD, HD), jnp.bfloat16), pltpu.VMEM((HD, HD), jnp.bfloat16)],
        compiler_params=pltpu.CompilerParams(vmem_limit_bytes=14 << 20),
        cost_estimate=pl.CostEstimate(flops=1 << 20, bytes_accessed=1 << 16, transcendentals=0),
        name="flash_second",
    )(*q_list, *state, *packs)


def merge_kernel(sizes, final, *refs):
    in_refs, out_refs = refs[: sum(sizes)], refs[sum(sizes) :]
    for size, out_ref in zip(sizes, out_refs):
        parts, in_refs = in_refs[:size], in_refs[size:]
        rows = parts[0].shape[0] - STAT
        packed = jnp.zeros((STAT, HD), jnp.float32)
        for b in range(rows // HD):
            levels = []
            for part in parts:
                stat = part[rows : rows + STAT, :].astype(jnp.float32)[3 * b : 3 * b + 3]
                flat = stat[0:1] + stat[1:2] + stat[2:3]
                levels.append(jnp.transpose(jnp.broadcast_to(flat, (HD, HD))))
            top = functools.reduce(jnp.maximum, levels)
            total = jnp.zeros((HD, HD), jnp.float32)
            acc = jnp.zeros((HD, HD), jnp.float32)
            for part, level in zip(parts, levels):
                share = jnp.exp2(level - top)
                total = total + share
                acc = acc + share * part[b * HD : (b + 1) * HD, :].astype(jnp.float32)
            out_ref[b * HD : (b + 1) * HD, :] = (acc / total).astype(jnp.bfloat16)
            packed = pack_level(top + jnp.log2(total), packed, b * HD)
        if not final:
            out_ref[rows : rows + STAT, :] = packed.astype(jnp.bfloat16)


def merge(groups, final=False):
    parts = [part for group in groups for part in group]
    rows = parts[0].shape[0] - (STAT if final else 0)
    return pl.pallas_call(
        functools.partial(merge_kernel, [len(group) for group in groups], final),
        out_shape=[jax.ShapeDtypeStruct((rows, HD), jnp.bfloat16)] * len(groups),
        in_specs=[VMEM] * len(parts),
        out_specs=[VMEM] * len(groups),
        compiler_params=pltpu.CompilerParams(vmem_limit_bytes=12 << 20),
        cost_estimate=pl.CostEstimate(flops=1 << 20, bytes_accessed=1 << 16, transcendentals=0),
        name="merge",
    )(*parts)


def project_kernel(chunks, *refs):
    pair_refs, (w_own, w_core, out_ref, left_ref) = refs[:chunks], refs[chunks:]
    my_z, my_x, _ = place()
    heads = left_ref.shape[3] // HD
    for i in range(chunks):
        home = lax.rem(my_z + i, chunks)
        for k in range(2):
            for h in range(heads):
                first = (k * heads + h) * 16
                left_ref[home, my_x ^ k, :, h * HD : (h + 1) * HD] = pair_refs[i][
                    first : first + 16, :
                ]
    left = left_ref[...].reshape(chunks * 32, heads * HD)
    width = w_own.shape[1]
    for k, w in enumerate((w_own, w_core)):
        terms = jnp.dot(left, w[...], preferred_element_type=jnp.float32)
        out_ref[:, :, k * width : (k + 1) * width] = terms.astype(jnp.bfloat16).reshape(
            chunks, 32, width
        )


def project(pairs, w_own, w_core):
    chunks = len(pairs)
    depth, width = w_own.shape
    return pl.pallas_call(
        functools.partial(project_kernel, chunks),
        out_shape=jax.ShapeDtypeStruct((chunks, 32, 2 * width), jnp.bfloat16),
        in_specs=[VMEM] * (chunks + 2),
        out_specs=VMEM,
        scratch_shapes=[pltpu.VMEM((chunks, 2, 16, depth), jnp.bfloat16)],
        compiler_params=pltpu.CompilerParams(vmem_limit_bytes=14 << 20),
        cost_estimate=pl.CostEstimate(
            flops=2 * chunks * 32 * depth * 2 * width, bytes_accessed=6 << 20, transcendentals=0
        ),
        name="project",
    )(*pairs, w_own, w_core)


def on_device(
    queries, cache_keys, cache_values, new_keys, new_values, fill_rows, turn_start, out_weight
):
    tok_dev, group_size, head_width = queries.shape
    ctx_count = lax.axis_size("ctx")
    shards = ctx_count // 4
    me = lax.axis_index("ctx")
    my_z, my_x, my_c = me // 4, (me // 2) % 2, me % 2
    cache_rows = cache_keys.shape[0]

    def permutation(dz, dx, dc):
        place = lambda z, x, c: ((z % shards) * 2 + x) * 2 + c
        return [
            (place(z, x, c), place(z + dz, x ^ dx, c ^ dc))
            for z in range(shards)
            for x in range(2)
            for c in range(2)
        ]

    def send(value, dz=0, dx=0, dc=0):
        return lax.ppermute(value, "ctx", permutation(dz, dx, dc))

    def after(value, *others):
        return lax.optimization_barrier((value,) + others)[0]

    positions = (turn_start[0] + me * tok_dev + jnp.arange(tok_dev, dtype=jnp.int32)).astype(
        jnp.float32
    )
    q = {}
    fresh = jnp.concatenate(
        [
            new_keys.reshape(tok_dev, head_width),
            new_values.reshape(tok_dev, head_width),
            jnp.full((16, head_width), fill_rows[0].astype(jnp.bfloat16)),
        ],
        axis=0,
    )
    q[0], pack = prepare(
        queries,
        cache_keys.reshape(cache_rows, head_width),
        cache_values.reshape(cache_rows, head_width),
        fresh,
        positions,
    )
    pack_x, pack_c = send(pack, dx=1), send(pack, dc=1)
    for d in (1, -1, 2, -2):
        q[d] = send(q[0], dz=-d)
    here, close, wide, outer = (0,), (1, -1), (2, -2), (3, -3, 4)
    state = {here: flash_first([q[0]], (pack, pack_c))}
    arrived = (q[1], q[-1], state[here][1])
    pack_x = after(pack_x, q[2], q[-2], *arrived)
    pack_xc = send(pack_x, dc=1)
    up, down = after(q[2], q[-2], *arrived), after(q[-2], q[2], *arrived)
    q[3], q[-3], q[4] = send(up, dz=-1), send(down, dz=1), send(up, dz=-2)
    both = flash_first([q[d] for d in close + wide], (pack, pack_c))
    state[close], state[wide] = both, both
    q[-3] = after(q[-3], both[1])
    state[outer] = flash_first([q[d] for d in outer], (pack, pack_c))
    packs = (pack, pack_c, pack_x, pack_xc)

    part = {}

    def finish(offsets, first=0):
        chunks = [q[d] for d in offsets]
        done = flash_second(offsets, shards, chunks, state[offsets], first, packs)
        part.update(zip(offsets, done))

    finish(outer)
    from_3, from_4, from_m3 = send(part[3], dz=1), send(part[4], dz=2), send(part[-3], dz=-1)
    finish(wide, 2)
    q[1] = after(q[1], part[2])
    finish(close)
    got = [send(part[1], dz=1), send(part[-1], dz=-1)]
    part[2] = after(part[2], part[1])
    up, down = merge([[part[2], from_3, from_4], [part[-2], from_m3]])
    got += [send(up, dz=2), send(down, dz=-2)]
    q[0] = after(q[0], up)
    finish(here)
    attention = merge([[part[0]] + got], final=True)[0]

    pair = {0: jnp.concatenate([attention, send(attention, dx=1)], axis=0)}
    for d in (1, -1, 2, -2):
        pair[d] = send(pair[0], dz=-d)
    pair[3], pair[-3], pair[4] = send(pair[2], dz=-1), send(pair[-2], dz=1), send(pair[2], dz=-2)
    w_core = send(out_weight, dc=1)
    terms = project([pair[d if d <= 4 else d - 8] for d in range(8)], out_weight, w_core)
    summed = (
        lax.all_to_all(terms, "kvh", 0, 0, tiled=True)
        .astype(jnp.float32)
        .sum(axis=0)
        .astype(jnp.bfloat16)
    )
    width = out_weight.shape[1]
    mine = summed[:, :width].reshape(2, 1, tok_dev, width)
    other = send(summed[:, width:], dc=1).reshape(2, 1, tok_dev, width)
    ordered = jnp.where(
        my_c == 0,
        jnp.concatenate([mine, other], axis=1),
        jnp.concatenate([other, mine], axis=1),
    )
    return ordered.reshape(4 * tok_dev, width)


def solution(mesh):
    in_specs = (
        P("ctx", "kvh", None),
        P("ctx", "kvh", None),
        P("ctx", "kvh", None),
        P("ctx", "kvh", None),
        P("ctx", "kvh", None),
        P("ctx"),
        P(),
        P("kvh", "ctx"),
    )
    out_specs = P("kvh", "ctx")
    return jax.shard_map(
        on_device, mesh=mesh, in_specs=in_specs, out_specs=out_specs, check_vma=False
    )
```

```python
import functools
import math

import jax
import jax.numpy as jnp
from jax import lax
from jax.experimental import pallas as pl
from jax.experimental.pallas import tpu as pltpu
from jax.sharding import PartitionSpec as P

NEG = -1e30
ROPE_BASE = 500000.0
LOG2E = 1.4426950408889634
HD = 128
STAT = 16
CTX = ("z", "x", "c")
VMEM = pl.BlockSpec(memory_space=pltpu.VMEM)
HBM = pl.BlockSpec(memory_space=pltpu.HBM)


def rotate_kernel(q_ref, cosine, sine, q_out, turned):
    tokens, heads, width = q_ref.shape
    cos, sin = cosine[...], sine[...]
    old = q_ref[...].astype(jnp.float32)
    swapped = pltpu.roll(old.reshape(tokens * heads, width), HD // 2, 1).reshape(old.shape)
    turned[...] = old * cos[:, None, :] + swapped * sin[:, None, :]
    for h in range(heads):
        q_out[tokens * h : tokens * (h + 1), :] = turned[:, h, :].astype(jnp.bfloat16)


def rotate(queries, cosine, sine):
    tokens, heads, width = queries.shape
    return pl.pallas_call(
        rotate_kernel,
        out_shape=jax.ShapeDtypeStruct((tokens * heads, width), jnp.bfloat16),
        in_specs=[VMEM] * 3,
        out_specs=VMEM,
        scratch_shapes=[pltpu.VMEM(queries.shape, jnp.float32)],
        compiler_params=pltpu.CompilerParams(vmem_limit_bytes=12 << 20),
        cost_estimate=pl.CostEstimate(flops=1 << 18, bytes_accessed=1 << 17, transcendentals=0),
        name="rotate",
    )(queries, cosine, sine)


def pack_kernel(k_hbm, v_hbm, fresh, cosine, sine, pack_out, sems):
    n = k_hbm.shape[0]
    piece = n // 4
    copies = []
    for i in range(8):
        source = (k_hbm, v_hbm)[i // 4].at[i % 4 * piece : (i % 4 + 1) * piece]
        target = pack_out.at[i * piece : (i + 1) * piece]
        copies.append(pltpu.make_async_copy(source, target, sems.at[i]))
    for copy in copies:
        copy.start()
    new_k = fresh[0:16, :].astype(jnp.float32)
    new_k = new_k * cosine[...] + pltpu.roll(new_k, HD // 2, 1) * sine[...]
    pack_out[2 * n : 2 * n + 16, :] = new_k.astype(jnp.bfloat16)
    pack_out[2 * n + 16 : 2 * n + NOTE, :] = fresh[16:NOTE, :]
    for copy in copies:
        copy.wait()


def pack_up(keys, values, fresh, cosine, sine):
    n, width = keys.shape
    return pl.pallas_call(
        pack_kernel,
        out_shape=jax.ShapeDtypeStruct((2 * n + NOTE, width), jnp.bfloat16),
        in_specs=[HBM] * 2 + [VMEM] * 3,
        out_specs=VMEM,
        scratch_shapes=[pltpu.SemaphoreType.DMA((8,))],
        compiler_params=pltpu.CompilerParams(vmem_limit_bytes=12 << 20),
        cost_estimate=pl.CostEstimate(flops=1 << 18, bytes_accessed=1 << 20, transcendentals=0),
        name="pack_up",
    )(keys, values, fresh, cosine, sine)


def turning(positions, width):
    steps_index = jnp.arange(width // 2, dtype=jnp.float32)
    inverse = jnp.exp(steps_index * (-2.0 * math.log(ROPE_BASE) / width))
    angles = positions[:, None] * jnp.concatenate([inverse, inverse])[None, :]
    sign = jnp.where(jnp.arange(width) < width // 2, -1.0, 1.0).astype(jnp.float32)
    return jnp.cos(angles), jnp.sin(angles) * sign


def dot_nt(a, b):
    return lax.dot_general(a, b, (((1,), (1,)), ((), ())), preferred_element_type=jnp.float32)


NOTE = 48


def fill_bias(pack, n):
    fill = pack[2 * n + 32 : 2 * n + 48, :].astype(jnp.float32)[0:1, :]
    fill = jnp.concatenate([fill] * (n // HD), axis=1)
    row = lax.broadcasted_iota(jnp.int32, (1, n), 1).astype(jnp.float32)
    return jnp.where(row < fill, 0.0, NEG)


def absorb(state, scores, values):
    weigh = jnp.concatenate([values, jnp.ones_like(values)], axis=1)
    high = scores.max(axis=1, keepdims=True)
    if state is None:
        weights = jnp.exp2(scores - high).astype(jnp.bfloat16)
        return high, jnp.dot(weights, weigh, preferred_element_type=jnp.float32)
    top, acc = state
    high = jnp.maximum(top, high)
    weights = jnp.exp2(scores - high).astype(jnp.bfloat16)
    term = jnp.dot(weights, weigh, preferred_element_type=jnp.float32)
    return high, acc * jnp.exp2(top - high) + term


def sweep(states, tiles, packs):
    scale = LOG2E / math.sqrt(HD)
    for pack in packs:
        n = (pack.shape[0] - NOTE) // 2
        block = min(512, n)
        bias = fill_bias(pack, n)
        for b in range(0, n, block):
            for t, q in enumerate(tiles):
                scores = dot_nt(q, pack[b : b + block, :]) * scale + bias[:, b : b + block]
                states[t] = absorb(states[t], scores, pack[n + b : n + b + block, :])
    return states


def tile_groups(q_refs):
    whole = q_refs[0].shape[0]
    even = len(q_refs) // 2 * 2
    groups = [((i, 0, whole), (i + 1, 0, whole)) for i in range(0, even, 2)]
    if even < len(q_refs):
        groups.append(((even, 0, whole // 2), (even, whole // 2, whole // 2)))
    return groups


def first_kernel(chunks, *refs):
    q_refs, refs = refs[:chunks], refs[chunks:]
    packs, (acc_ref, top_ref) = refs[0:2], refs[2:]
    for group in tile_groups(q_refs):
        tiles = [q_refs[i][p : p + rows, :] for i, p, rows in group]
        states = sweep([None] * len(tiles), tiles, packs)
        for (i, p, rows), (top, acc) in zip(group, states):
            acc_ref[i, p : p + rows, :] = acc
            top_ref[i, p : p + rows, :] = jnp.broadcast_to(top, (rows, HD))


def flash_first(q_list, packs):
    chunks, rows = len(q_list), q_list[0].shape[0]
    keys = sum(pack.shape[0] - NOTE for pack in packs) // 2
    return pl.pallas_call(
        functools.partial(first_kernel, chunks),
        out_shape=(
            jax.ShapeDtypeStruct((chunks, rows, 2 * HD), jnp.float32),
            jax.ShapeDtypeStruct((chunks, rows, HD), jnp.float32),
        ),
        in_specs=[VMEM] * (chunks + 2),
        out_specs=(VMEM, VMEM),
        compiler_params=pltpu.CompilerParams(vmem_limit_bytes=14 << 20),
        cost_estimate=pl.CostEstimate(
            flops=chunks << 29, bytes_accessed=1 << 20, transcendentals=0
        ),
        name="flash_first",
    )(*q_list, *packs)


def pack_level(level, stat, first_row):
    line = lax.broadcasted_iota(jnp.int32, stat.shape, 0)
    for b in range(level.shape[0] // HD):
        flat = jnp.transpose(level[b * HD : (b + 1) * HD, :])[0:STAT, :]
        for t in range(3):
            piece = flat.astype(jnp.bfloat16).astype(jnp.float32)
            stat = jnp.where(line == 3 * (first_row // HD + b) + t, piece, stat)
            flat = flat - piece
    return stat


def place():
    return lax.axis_index("z"), lax.axis_index("x"), lax.axis_index("c")


def second_kernel(offsets, shards, first, *refs):
    chunks = len(offsets)
    q_refs, refs = refs[:chunks], refs[chunks:]
    acc_ref, top_ref, packs = refs[0], refs[1], refs[2:6]
    out_refs, (new_k, new_v) = refs[6 : 6 + chunks], refs[6 + chunks :]
    n = (packs[0].shape[0] - NOTE) // 2
    new_k[...] = jnp.zeros_like(new_k)
    new_v[...] = jnp.zeros_like(new_v)
    for s, pack in enumerate(packs):
        new_k[16 * s : 16 * s + 16, :] = pack[2 * n : 2 * n + 16, :]
        new_v[16 * s : 16 * s + 16, :] = pack[2 * n + 16 : 2 * n + 32, :]
    scale = LOG2E / math.sqrt(HD)
    my_z, my_x, my_c = place()
    column = lax.broadcasted_iota(jnp.int32, (1, HD), 1)
    key_token = (
        64 * my_z
        + 32 * (my_x ^ (column >> 5))
        + 16 * (my_c ^ ((column >> 4) & 1))
        + (column & 15)
    )
    key_token = jnp.where(column < 64, key_token, 1 << 20)
    stats = [jnp.zeros((STAT, HD), jnp.float32) for _ in q_refs]
    for group in tile_groups(q_refs):
        tiles = [q_refs[i][p : p + rows, :] for i, p, rows in group]
        states = []
        for tile, (i, p, rows) in zip(tiles, group):
            home = lax.rem(my_z + offsets[i] + shards, shards)
            row_token = lax.broadcasted_iota(jnp.int32, (rows, HD), 0) & 15
            row_token = row_token + (64 * home + 32 * my_x + 16 * my_c)
            scores = dot_nt(tile, new_k[...]) * scale
            scores = jnp.where(key_token <= row_token, scores, NEG)
            states.append(absorb(None, scores, new_v[...]))
        states = sweep(states, tiles, packs[2:])
        for (i, p, rows), (top, acc) in zip(group, states):
            near_top = top_ref[first + i, p : p + rows, :]
            top = jnp.broadcast_to(top, near_top.shape)
            high = jnp.maximum(top, near_top)
            near, far = jnp.exp2(near_top - high), jnp.exp2(top - high)
            near_acc = acc_ref[first + i, p : p + rows, :]
            total = near * near_acc[:, HD:] + far * acc[:, HD:]
            mean = (near * near_acc[:, :HD] + far * acc[:, :HD]) / total
            out_refs[i][p : p + rows, :] = mean.astype(jnp.bfloat16)
            stats[i] = pack_level(high + jnp.log2(total), stats[i], p)
    for i, out in enumerate(out_refs):
        whole = q_refs[i].shape[0]
        out[whole : whole + STAT, :] = stats[i].astype(jnp.bfloat16)


def flash_second(offsets, shards, q_list, state, first, packs):
    chunks, rows = len(q_list), q_list[0].shape[0]
    keys = packs[0].shape[0]
    return pl.pallas_call(
        functools.partial(second_kernel, offsets, shards, first),
        out_shape=[jax.ShapeDtypeStruct((rows + STAT, HD), jnp.bfloat16)] * chunks,
        in_specs=[VMEM] * (chunks + 6),
        out_specs=[VMEM] * chunks,
        scratch_shapes=[pltpu.VMEM((HD, HD), jnp.bfloat16), pltpu.VMEM((HD, HD), jnp.bfloat16)],
        compiler_params=pltpu.CompilerParams(vmem_limit_bytes=14 << 20),
        cost_estimate=pl.CostEstimate(flops=1 << 20, bytes_accessed=1 << 16, transcendentals=0),
        name="flash_second",
    )(*q_list, *state, *packs)


def merge_kernel(sizes, final, *refs):
    in_refs, out_refs = refs[: sum(sizes)], refs[sum(sizes) :]
    for size, out_ref in zip(sizes, out_refs):
        parts, in_refs = in_refs[:size], in_refs[size:]
        rows = parts[0].shape[0] - STAT
        packed = jnp.zeros((STAT, HD), jnp.float32)
        for b in range(rows // HD):
            levels = []
            for part in parts:
                stat = part[rows : rows + STAT, :].astype(jnp.float32)[3 * b : 3 * b + 3]
                flat = stat[0:1] + stat[1:2] + stat[2:3]
                levels.append(jnp.transpose(jnp.broadcast_to(flat, (HD, HD))))
            top = functools.reduce(jnp.maximum, levels)
            total = jnp.zeros((HD, HD), jnp.float32)
            acc = jnp.zeros((HD, HD), jnp.float32)
            for part, level in zip(parts, levels):
                share = jnp.exp2(level - top)
                total = total + share
                acc = acc + share * part[b * HD : (b + 1) * HD, :].astype(jnp.float32)
            out_ref[b * HD : (b + 1) * HD, :] = (acc / total).astype(jnp.bfloat16)
            packed = pack_level(top + jnp.log2(total), packed, b * HD)
        if not final:
            out_ref[rows : rows + STAT, :] = packed.astype(jnp.bfloat16)


def merge(groups, final=False):
    parts = [part for group in groups for part in group]
    rows = parts[0].shape[0] - (STAT if final else 0)
    return pl.pallas_call(
        functools.partial(merge_kernel, [len(group) for group in groups], final),
        out_shape=[jax.ShapeDtypeStruct((rows, HD), jnp.bfloat16)] * len(groups),
        in_specs=[VMEM] * len(parts),
        out_specs=[VMEM] * len(groups),
        compiler_params=pltpu.CompilerParams(vmem_limit_bytes=12 << 20),
        cost_estimate=pl.CostEstimate(flops=1 << 20, bytes_accessed=1 << 16, transcendentals=0),
        name="merge",
    )(*parts)


def project_kernel(chunks, *refs):
    pair_refs, (w_own, w_core, out_ref, left_ref) = refs[:chunks], refs[chunks:]
    my_z, my_x, my_c = place()
    heads = left_ref.shape[3] // HD
    for i in range(chunks):
        home = lax.rem(my_z + i, chunks)
        for k in range(2):
            for h in range(heads):
                first = (k * heads + h) * 16
                left_ref[home, my_x ^ k, :, h * HD : (h + 1) * HD] = pair_refs[i][
                    first : first + 16, :
                ]
    left = left_ref[...].reshape(chunks * 32, heads * HD)
    for k, w in enumerate((w_own, w_core)):
        terms = jnp.dot(left, w[...], preferred_element_type=jnp.float32)
        out_ref[my_c ^ k] = terms.astype(jnp.bfloat16).reshape(chunks, 32, w.shape[1])


def project(pairs, w_own, w_core):
    chunks = len(pairs)
    depth, width = w_own.shape
    return pl.pallas_call(
        functools.partial(project_kernel, chunks),
        out_shape=jax.ShapeDtypeStruct((2, chunks, 32, width), jnp.bfloat16),
        in_specs=[VMEM] * (chunks + 2),
        out_specs=VMEM,
        scratch_shapes=[pltpu.VMEM((chunks, 2, 16, depth), jnp.bfloat16)],
        compiler_params=pltpu.CompilerParams(vmem_limit_bytes=14 << 20),
        cost_estimate=pl.CostEstimate(
            flops=2 * chunks * 32 * depth * 2 * width, bytes_accessed=6 << 20, transcendentals=0
        ),
        name="project",
    )(*pairs, w_own, w_core)


def total_kernel(in_ref, out_ref):
    shards = in_ref.shape[0] // 2
    for c in range(2):
        acc = in_ref[c * shards].astype(jnp.float32)
        for g in range(1, shards):
            acc = acc + in_ref[c * shards + g].astype(jnp.float32)
        for x in range(2):
            first = (2 * x + c) * 16
            out_ref[first : first + 16, :] = acc[16 * x : 16 * x + 16].astype(jnp.bfloat16)


def total(got):
    return pl.pallas_call(
        total_kernel,
        out_shape=jax.ShapeDtypeStruct((64, got.shape[2]), jnp.bfloat16),
        in_specs=[VMEM],
        out_specs=VMEM,
        compiler_params=pltpu.CompilerParams(vmem_limit_bytes=8 << 20),
        cost_estimate=pl.CostEstimate(flops=1 << 18, bytes_accessed=1 << 19, transcendentals=0),
        name="total",
    )(got)


def on_device(
    queries, cache_keys, cache_values, new_keys, new_values, fill_rows, turn_start, out_weight
):
    tok_dev, group_size, head_width = queries.shape
    shards = lax.axis_size("z")
    me = lax.axis_index(CTX)
    cache_rows = cache_keys.shape[0]

    def permutation(dz, dx, dc):
        place = lambda z, x, c: ((z % shards) * 2 + x) * 2 + c
        return [
            (place(z, x, c), place(z + dz, x ^ dx, c ^ dc))
            for z in range(shards)
            for x in range(2)
            for c in range(2)
        ]

    def send(value, dz=0, dx=0, dc=0):
        return lax.ppermute(value, CTX, permutation(dz, dx, dc))

    def after(value, *others):
        return lax.optimization_barrier((value,) + others)[0]

    positions = (turn_start[0] + me * tok_dev + jnp.arange(tok_dev, dtype=jnp.int32)).astype(
        jnp.float32
    )
    cosine, sine = turning(positions, head_width)
    q = {0: rotate(queries, cosine, sine)}
    fresh = jnp.concatenate(
        [
            new_keys.reshape(tok_dev, head_width),
            new_values.reshape(tok_dev, head_width),
            jnp.full((16, head_width), fill_rows[0].astype(jnp.bfloat16)),
        ],
        axis=0,
    )
    pack = pack_up(
        cache_keys.reshape(cache_rows, head_width),
        cache_values.reshape(cache_rows, head_width),
        after(fresh, q[0]),
        cosine,
        sine,
    )
    pack_x = send(pack, dx=1)
    for d in (1, -1, 2, -2):
        q[d] = send(q[0], dz=-d)
    here, close, wide, outer = (0,), (1, -1), (2, -2), (3, -3, 4)
    arrived = (q[1], q[-1], q[2], q[-2])
    pack_c, pack_xc = send(after(pack, *arrived), dc=1), send(after(pack_x, *arrived), dc=1)
    up, down = after(q[2], *arrived), after(q[-2], *arrived)
    q[3], q[-3], q[4] = send(up, dz=-1), send(down, dz=1), send(up, dz=-2)
    state = {here: flash_first([q[0]], (pack, pack_c))}
    both = flash_first([q[d] for d in close + wide], (pack, pack_c))
    state[close], state[wide] = both, both
    q[-3] = after(q[-3], both[1], state[here][1])
    state[outer] = flash_first([q[d] for d in outer], (pack, pack_c))
    packs = (pack, pack_c, pack_x, pack_xc)

    part = {}

    def finish(offsets, first=0):
        chunks = [q[d] for d in offsets]
        done = flash_second(offsets, shards, chunks, state[offsets], first, packs)
        part.update(zip(offsets, done))

    finish(outer)
    from_3, from_4, from_m3 = send(part[3], dz=1), send(part[4], dz=2), send(part[-3], dz=-1)
    finish(wide, 2)
    q[1] = after(q[1], part[2])
    finish(close)
    got = [send(part[1], dz=1), send(part[-1], dz=-1)]
    part[2] = after(part[2], part[1])
    up, down = merge([[part[2], from_3, from_4], [part[-2], from_m3]])
    got += [send(up, dz=2), send(down, dz=-2)]
    q[0] = after(q[0], up)
    finish(here)
    attention = merge([[part[0]] + got], final=True)[0]

    pair = {0: jnp.concatenate([attention, send(attention, dx=1)], axis=0)}
    for d in (1, -1, 2, -2):
        pair[d] = send(pair[0], dz=-d)
    pair[3], pair[-3], pair[4] = send(pair[2], dz=-1), send(pair[-2], dz=1), send(pair[2], dz=-2)
    w_core = send(out_weight, dc=1)
    terms = project([pair[d if d <= 4 else d - 8] for d in range(8)], out_weight, w_core)
    width = out_weight.shape[1]
    terms = terms.reshape(2 * shards, 2 * tok_dev, width)
    got = lax.all_to_all(terms, ("c", "kvh"), 0, 0, tiled=True)
    return total(got)


def solution(mesh):
    shape = (mesh.shape["ctx"] // 4, 2, 2, mesh.shape["kvh"])
    fine = jax.sharding.Mesh(mesh.devices.reshape(shape), CTX + ("kvh",))
    split = P(CTX, "kvh", None)
    in_specs = (split, split, split, split, split, P(CTX), P(), P("kvh", CTX))
    return jax.shard_map(
        on_device, mesh=fine, in_specs=in_specs, out_specs=P("kvh", CTX), check_vma=False
    )
```

```python
import functools
import math

import jax
import jax.numpy as jnp
from jax import lax
from jax.experimental import pallas as pl
from jax.experimental.pallas import tpu as pltpu
from jax.sharding import PartitionSpec as P

NEG = -1e30
ROPE_BASE = 500000.0
LOG2E = 1.4426950408889634
HD = 128
STAT = 16
CTX = ("z", "x", "c")
VMEM = pl.BlockSpec(memory_space=pltpu.VMEM)
HBM = pl.BlockSpec(memory_space=pltpu.HBM)


def rotate_kernel(q_ref, cosine, sine, q_out, turned):
    tokens, heads, width = q_ref.shape
    cos, sin = cosine[...], sine[...]
    old = q_ref[...].astype(jnp.float32)
    swapped = pltpu.roll(old.reshape(tokens * heads, width), HD // 2, 1).reshape(old.shape)
    turned[...] = old * cos[:, None, :] + swapped * sin[:, None, :]
    for h in range(heads):
        q_out[tokens * h : tokens * (h + 1), :] = turned[:, h, :].astype(jnp.bfloat16)


def rotate(queries, cosine, sine):
    tokens, heads, width = queries.shape
    return pl.pallas_call(
        rotate_kernel,
        out_shape=jax.ShapeDtypeStruct((tokens * heads, width), jnp.bfloat16),
        in_specs=[VMEM] * 3,
        out_specs=VMEM,
        scratch_shapes=[pltpu.VMEM(queries.shape, jnp.float32)],
        compiler_params=pltpu.CompilerParams(vmem_limit_bytes=12 << 20),
        cost_estimate=pl.CostEstimate(flops=1 << 18, bytes_accessed=1 << 17, transcendentals=0),
        name="rotate",
    )(queries, cosine, sine)


def pack_kernel(k_hbm, v_hbm, fresh, cosine, sine, pack_out, sems):
    n = k_hbm.shape[0]
    piece = n // 4
    copies = []
    for i in range(8):
        source = (k_hbm, v_hbm)[i // 4].at[i % 4 * piece : (i % 4 + 1) * piece]
        target = pack_out.at[i * piece : (i + 1) * piece]
        copies.append(pltpu.make_async_copy(source, target, sems.at[i]))
    for copy in copies:
        copy.start()
    new_k = fresh[0:16, :].astype(jnp.float32)
    new_k = new_k * cosine[...] + pltpu.roll(new_k, HD // 2, 1) * sine[...]
    pack_out[2 * n : 2 * n + 16, :] = new_k.astype(jnp.bfloat16)
    pack_out[2 * n + 16 : 2 * n + NOTE, :] = fresh[16:NOTE, :]
    for copy in copies:
        copy.wait()


def pack_up(keys, values, fresh, cosine, sine):
    n, width = keys.shape
    return pl.pallas_call(
        pack_kernel,
        out_shape=jax.ShapeDtypeStruct((2 * n + NOTE, width), jnp.bfloat16),
        in_specs=[HBM] * 2 + [VMEM] * 3,
        out_specs=VMEM,
        scratch_shapes=[pltpu.SemaphoreType.DMA((8,))],
        compiler_params=pltpu.CompilerParams(vmem_limit_bytes=12 << 20),
        cost_estimate=pl.CostEstimate(flops=1 << 18, bytes_accessed=1 << 20, transcendentals=0),
        name="pack_up",
    )(keys, values, fresh, cosine, sine)


def turning(positions, width):
    steps_index = jnp.arange(width // 2, dtype=jnp.float32)
    inverse = jnp.exp(steps_index * (-2.0 * math.log(ROPE_BASE) / width))
    angles = positions[:, None] * jnp.concatenate([inverse, inverse])[None, :]
    sign = jnp.where(jnp.arange(width) < width // 2, -1.0, 1.0).astype(jnp.float32)
    return jnp.cos(angles), jnp.sin(angles) * sign


def dot_nt(a, b):
    return lax.dot_general(a, b, (((1,), (1,)), ((), ())), preferred_element_type=jnp.float32)


NOTE = 48


def fill_bias(pack, n):
    fill = pack[2 * n + 32 : 2 * n + 48, :].astype(jnp.float32)[0:1, :]
    fill = jnp.concatenate([fill] * (n // HD), axis=1)
    row = lax.broadcasted_iota(jnp.int32, (1, n), 1).astype(jnp.float32)
    return jnp.where(row < fill, 0.0, NEG)


def absorb(state, scores, values):
    weigh = jnp.concatenate([values, jnp.ones_like(values)], axis=1)
    high = scores.max(axis=1, keepdims=True)
    if state is None:
        weights = jnp.exp2(scores - high).astype(jnp.bfloat16)
        return high, jnp.dot(weights, weigh, preferred_element_type=jnp.float32)
    top, acc = state
    high = jnp.maximum(top, high)
    weights = jnp.exp2(scores - high).astype(jnp.bfloat16)
    term = jnp.dot(weights, weigh, preferred_element_type=jnp.float32)
    return high, acc * jnp.exp2(top - high) + term


def sweep(states, tiles, packs):
    scale = LOG2E / math.sqrt(HD)
    for pack in packs:
        n = (pack.shape[0] - NOTE) // 2
        block = min(512, n)
        bias = fill_bias(pack, n)
        for b in range(0, n, block):
            for t, q in enumerate(tiles):
                scores = dot_nt(q, pack[b : b + block, :]) * scale + bias[:, b : b + block]
                states[t] = absorb(states[t], scores, pack[n + b : n + b + block, :])
    return states


def tile_groups(q_refs):
    whole = q_refs[0].shape[0]
    even = len(q_refs) // 2 * 2
    groups = [((i, 0, whole), (i + 1, 0, whole)) for i in range(0, even, 2)]
    if even < len(q_refs):
        groups.append(((even, 0, whole // 2), (even, whole // 2, whole // 2)))
    return groups


def first_kernel(chunks, *refs):
    q_refs, refs = refs[:chunks], refs[chunks:]
    packs, (acc_ref, top_ref) = refs[0:2], refs[2:]
    for group in tile_groups(q_refs):
        tiles = [q_refs[i][p : p + rows, :] for i, p, rows in group]
        states = sweep([None] * len(tiles), tiles, packs)
        for (i, p, rows), (top, acc) in zip(group, states):
            acc_ref[i, p : p + rows, :] = acc
            top_ref[i, p : p + rows, :] = jnp.broadcast_to(top, (rows, HD))


def flash_first(q_list, packs):
    chunks, rows = len(q_list), q_list[0].shape[0]
    keys = sum(pack.shape[0] - NOTE for pack in packs) // 2
    return pl.pallas_call(
        functools.partial(first_kernel, chunks),
        out_shape=(
            jax.ShapeDtypeStruct((chunks, rows, 2 * HD), jnp.float32),
            jax.ShapeDtypeStruct((chunks, rows, HD), jnp.float32),
        ),
        in_specs=[VMEM] * (chunks + 2),
        out_specs=(VMEM, VMEM),
        compiler_params=pltpu.CompilerParams(vmem_limit_bytes=14 << 20),
        cost_estimate=pl.CostEstimate(
            flops=chunks << 29, bytes_accessed=1 << 20, transcendentals=0
        ),
        name="flash_first",
    )(*q_list, *packs)


def pack_level(level, stat, first_row):
    line = lax.broadcasted_iota(jnp.int32, stat.shape, 0)
    for b in range(level.shape[0] // HD):
        flat = jnp.transpose(level[b * HD : (b + 1) * HD, :])[0:STAT, :]
        for t in range(3):
            piece = flat.astype(jnp.bfloat16).astype(jnp.float32)
            stat = jnp.where(line == 3 * (first_row // HD + b) + t, piece, stat)
            flat = flat - piece
    return stat


def place():
    return lax.axis_index("z"), lax.axis_index("x"), lax.axis_index("c")


def second_kernel(offsets, shards, first, *refs):
    chunks = len(offsets)
    q_refs, refs = refs[:chunks], refs[chunks:]
    acc_ref, top_ref, packs = refs[0], refs[1], refs[2:6]
    out_refs, (new_k, new_v) = refs[6 : 6 + chunks], refs[6 + chunks :]
    n = (packs[0].shape[0] - NOTE) // 2
    new_k[...] = jnp.zeros_like(new_k)
    new_v[...] = jnp.zeros_like(new_v)
    for s, pack in enumerate(packs):
        new_k[16 * s : 16 * s + 16, :] = pack[2 * n : 2 * n + 16, :]
        new_v[16 * s : 16 * s + 16, :] = pack[2 * n + 16 : 2 * n + 32, :]
    scale = LOG2E / math.sqrt(HD)
    my_z, my_x, my_c = place()
    column = lax.broadcasted_iota(jnp.int32, (1, HD), 1)
    key_token = (
        64 * my_z
        + 32 * (my_x ^ (column >> 5))
        + 16 * (my_c ^ ((column >> 4) & 1))
        + (column & 15)
    )
    key_token = jnp.where(column < 64, key_token, 1 << 20)
    stats = [jnp.zeros((STAT, HD), jnp.float32) for _ in q_refs]
    for group in tile_groups(q_refs):
        tiles = [q_refs[i][p : p + rows, :] for i, p, rows in group]
        states = []
        for tile, (i, p, rows) in zip(tiles, group):
            home = lax.rem(my_z + offsets[i] + shards, shards)
            row_token = lax.broadcasted_iota(jnp.int32, (rows, HD), 0) & 15
            row_token = row_token + (64 * home + 32 * my_x + 16 * my_c)
            scores = dot_nt(tile, new_k[...]) * scale
            scores = jnp.where(key_token <= row_token, scores, NEG)
            states.append(absorb(None, scores, new_v[...]))
        states = sweep(states, tiles, packs[2:])
        for (i, p, rows), (top, acc) in zip(group, states):
            near_top = top_ref[first + i, p : p + rows, :]
            top = jnp.broadcast_to(top, near_top.shape)
            high = jnp.maximum(top, near_top)
            near, far = jnp.exp2(near_top - high), jnp.exp2(top - high)
            near_acc = acc_ref[first + i, p : p + rows, :]
            total = near * near_acc[:, HD:] + far * acc[:, HD:]
            mean = (near * near_acc[:, :HD] + far * acc[:, :HD]) / total
            out_refs[i][p : p + rows, :] = mean.astype(jnp.bfloat16)
            stats[i] = pack_level(high + jnp.log2(total), stats[i], p)
    for i, out in enumerate(out_refs):
        whole = q_refs[i].shape[0]
        out[whole : whole + STAT, :] = stats[i].astype(jnp.bfloat16)


def flash_second(offsets, shards, q_list, state, first, packs):
    chunks, rows = len(q_list), q_list[0].shape[0]
    keys = packs[0].shape[0]
    return pl.pallas_call(
        functools.partial(second_kernel, offsets, shards, first),
        out_shape=[jax.ShapeDtypeStruct((rows + STAT, HD), jnp.bfloat16)] * chunks,
        in_specs=[VMEM] * (chunks + 6),
        out_specs=[VMEM] * chunks,
        scratch_shapes=[pltpu.VMEM((HD, HD), jnp.bfloat16), pltpu.VMEM((HD, HD), jnp.bfloat16)],
        compiler_params=pltpu.CompilerParams(vmem_limit_bytes=14 << 20),
        cost_estimate=pl.CostEstimate(flops=1 << 20, bytes_accessed=1 << 16, transcendentals=0),
        name="flash_second",
    )(*q_list, *state, *packs)


def merge_kernel(sizes, final, *refs):
    in_refs, out_refs = refs[: sum(sizes)], refs[sum(sizes) :]
    for size, out_ref in zip(sizes, out_refs):
        parts, in_refs = in_refs[:size], in_refs[size:]
        rows = parts[0].shape[0] - STAT
        packed = jnp.zeros((STAT, HD), jnp.float32)
        for b in range(rows // HD):
            levels = []
            for part in parts:
                stat = part[rows : rows + STAT, :].astype(jnp.float32)[3 * b : 3 * b + 3]
                flat = stat[0:1] + stat[1:2] + stat[2:3]
                levels.append(jnp.transpose(jnp.broadcast_to(flat, (HD, HD))))
            top = functools.reduce(jnp.maximum, levels)
            total = jnp.zeros((HD, HD), jnp.float32)
            acc = jnp.zeros((HD, HD), jnp.float32)
            for part, level in zip(parts, levels):
                share = jnp.exp2(level - top)
                total = total + share
                acc = acc + share * part[b * HD : (b + 1) * HD, :].astype(jnp.float32)
            out_ref[b * HD : (b + 1) * HD, :] = (acc / total).astype(jnp.bfloat16)
            packed = pack_level(top + jnp.log2(total), packed, b * HD)
        if not final:
            out_ref[rows : rows + STAT, :] = packed.astype(jnp.bfloat16)


def merge(groups, final=False):
    parts = [part for group in groups for part in group]
    rows = parts[0].shape[0] - (STAT if final else 0)
    return pl.pallas_call(
        functools.partial(merge_kernel, [len(group) for group in groups], final),
        out_shape=[jax.ShapeDtypeStruct((rows, HD), jnp.bfloat16)] * len(groups),
        in_specs=[VMEM] * len(parts),
        out_specs=[VMEM] * len(groups),
        compiler_params=pltpu.CompilerParams(vmem_limit_bytes=12 << 20),
        cost_estimate=pl.CostEstimate(flops=1 << 20, bytes_accessed=1 << 16, transcendentals=0),
        name="merge",
    )(*parts)


def project_kernel(chunks, *refs):
    pair_refs, (w_own, w_core, out_ref, left_ref) = refs[:chunks], refs[chunks:]
    my_z, my_x, my_c = place()
    heads = left_ref.shape[3] // HD
    for i in range(chunks):
        home = lax.rem(my_z + i, chunks)
        for k in range(2):
            for h in range(heads):
                first = (k * heads + h) * 16
                left_ref[home, my_x ^ k, :, h * HD : (h + 1) * HD] = pair_refs[i][
                    first : first + 16, :
                ]
    left = left_ref[...].reshape(chunks * 32, heads * HD)
    for k, w in enumerate((w_own, w_core)):
        terms = jnp.dot(left, w[...], preferred_element_type=jnp.float32)
        out_ref[my_c ^ k] = terms.astype(jnp.bfloat16).reshape(chunks, 32, w.shape[1])


def project(pairs, w_own, w_core):
    chunks = len(pairs)
    depth, width = w_own.shape
    return pl.pallas_call(
        functools.partial(project_kernel, chunks),
        out_shape=jax.ShapeDtypeStruct((2, chunks, 32, width), jnp.bfloat16),
        in_specs=[VMEM] * (chunks + 2),
        out_specs=VMEM,
        scratch_shapes=[pltpu.VMEM((chunks, 2, 16, depth), jnp.bfloat16)],
        compiler_params=pltpu.CompilerParams(vmem_limit_bytes=14 << 20),
        cost_estimate=pl.CostEstimate(
            flops=2 * chunks * 32 * depth * 2 * width, bytes_accessed=6 << 20, transcendentals=0
        ),
        name="project",
    )(*pairs, w_own, w_core)


def total_kernel(in_ref, out_ref):
    shards = in_ref.shape[0] // 2
    for c in range(2):
        acc = in_ref[c * shards].astype(jnp.float32)
        for g in range(1, shards):
            acc = acc + in_ref[c * shards + g].astype(jnp.float32)
        for x in range(2):
            first = (2 * x + c) * 16
            out_ref[first : first + 16, :] = acc[16 * x : 16 * x + 16].astype(jnp.bfloat16)


def total(got):
    return pl.pallas_call(
        total_kernel,
        out_shape=jax.ShapeDtypeStruct((64, got.shape[2]), jnp.bfloat16),
        in_specs=[VMEM],
        out_specs=VMEM,
        compiler_params=pltpu.CompilerParams(vmem_limit_bytes=8 << 20),
        cost_estimate=pl.CostEstimate(flops=1 << 18, bytes_accessed=1 << 19, transcendentals=0),
        name="total",
    )(got)


def on_device(
    queries, cache_keys, cache_values, new_keys, new_values, fill_rows, turn_start, out_weight
):
    tok_dev, group_size, head_width = queries.shape
    shards = lax.axis_size("z")
    me = lax.axis_index(CTX)
    cache_rows = cache_keys.shape[0]

    def permutation(dz, dx, dc):
        place = lambda z, x, c: ((z % shards) * 2 + x) * 2 + c
        return [
            (place(z, x, c), place(z + dz, x ^ dx, c ^ dc))
            for z in range(shards)
            for x in range(2)
            for c in range(2)
        ]

    def send(value, dz=0, dx=0, dc=0):
        return lax.ppermute(value, CTX, permutation(dz, dx, dc))

    def after(value, *others):
        return lax.optimization_barrier((value,) + others)[0]

    positions = (turn_start[0] + me * tok_dev + jnp.arange(tok_dev, dtype=jnp.int32)).astype(
        jnp.float32
    )
    cosine, sine = turning(positions, head_width)
    q = {0: rotate(queries, cosine, sine)}
    for d in (2, -2, 1, -1):
        q[d] = send(q[0], dz=-d)
    fresh = jnp.concatenate(
        [
            new_keys.reshape(tok_dev, head_width),
            new_values.reshape(tok_dev, head_width),
            jnp.full((16, head_width), fill_rows[0].astype(jnp.bfloat16)),
        ],
        axis=0,
    )
    pack = pack_up(
        cache_keys.reshape(cache_rows, head_width),
        cache_values.reshape(cache_rows, head_width),
        after(fresh, q[2], q[-2]),
        cosine,
        sine,
    )
    pack_x, pack_c = send(pack, dx=1), send(pack, dc=1)
    here, close, wide, outer = (0,), (1, -1), (2, -2), (3, -3, 4)
    q[3], q[-3], q[4] = send(q[2], dz=-1), send(q[-2], dz=1), send(q[2], dz=-2)
    state = {here: flash_first([q[0]], (pack, pack_c))}
    both = flash_first([q[d] for d in close + wide], (pack, pack_c))
    state[close], state[wide] = both, both
    pack_x = after(pack_x, both[1], state[here][1], q[3], q[-3], q[4])
    pack_xc = send(pack_x, dc=1)
    state[outer] = flash_first([q[d] for d in outer], (pack, pack_c))
    packs = (pack, pack_c, pack_x, pack_xc)

    part = {}

    def finish(offsets, first=0):
        chunks = [q[d] for d in offsets]
        done = flash_second(offsets, shards, chunks, state[offsets], first, packs)
        part.update(zip(offsets, done))

    finish(outer)
    from_3, from_4, from_m3 = send(part[3], dz=1), send(part[4], dz=2), send(part[-3], dz=-1)
    finish(wide, 2)
    q[1] = after(q[1], part[2])
    finish(close)
    got = [send(part[1], dz=1), send(part[-1], dz=-1)]
    part[2] = after(part[2], part[1])
    up, down = merge([[part[2], from_3, from_4], [part[-2], from_m3]])
    got += [send(up, dz=2), send(down, dz=-2)]
    q[0] = after(q[0], up)
    finish(here)
    attention = merge([[part[0]] + got], final=True)[0]

    pair = {0: jnp.concatenate([attention, send(attention, dx=1)], axis=0)}
    for d in (1, -1, 2, -2):
        pair[d] = send(pair[0], dz=-d)
    pair[3], pair[-3], pair[4] = send(pair[2], dz=-1), send(pair[-2], dz=1), send(pair[2], dz=-2)
    w_core = send(out_weight, dc=1)
    terms = project([pair[d if d <= 4 else d - 8] for d in range(8)], out_weight, w_core)
    width = out_weight.shape[1]
    terms = terms.reshape(2 * shards, 2 * tok_dev, width)
    got = lax.all_to_all(terms, ("c", "kvh"), 0, 0, tiled=True)
    return total(got)


def solution(mesh):
    shape = (mesh.shape["ctx"] // 4, 2, 2, mesh.shape["kvh"])
    fine = jax.sharding.Mesh(mesh.devices.reshape(shape), CTX + ("kvh",))
    split = P(CTX, "kvh", None)
    in_specs = (split, split, split, split, split, P(CTX), P(), P("kvh", CTX))
    return jax.shard_map(
        on_device, mesh=fine, in_specs=in_specs, out_specs=P("kvh", CTX), check_vma=False
    )
```
